32 devices in a mesh: dp: 16 (over z, x, core), tensor: 2 (over y).
Axes of the slice: x: 2, y: 2, z: 4, core: 2. Of those that a mesh axis runs over, the one named last changes fastest.
Arguments:
- inputs: bfloat16 [16384, 1024], P(('dp', 'tensor')), may hold values from -6 to 6
- attn_gain: float32 [1024], replicated, may hold values from 0.25 to 1.75
- attn_bias: float32 [1024], replicated, may hold values from -4 to 4
- mlp_gain: float32 [1024], replicated, may hold values from 0.25 to 1.75
- mlp_bias: float32 [1024], replicated, may hold values from -4 to 4
- w_qkv: bfloat16 [1024, 3072], P('dp', 'tensor'), may hold values from -0.1875 to 0.1875
- b_qkv: float32 [3072], P('tensor'), may hold values from -4 to 4
- w_out: bfloat16 [1024, 1024], P('tensor', 'dp'), may hold values from -2 to 2
- b_out: float32 [1024], replicated, may hold values from -4 to 4
- w_up: bfloat16 [1024, 4096], P('dp', 'tensor'), may hold values from -0.1875 to 0.1875
- b_up: float32 [4096], P('tensor'), may hold values from -4 to 4
- w_down: bfloat16 [4096, 1024], P('tensor', 'dp'), may hold values from -0.09375 to 0.09375
- b_down: float32 [1024], replicated, may hold values from -4 to 4
- cotangent: bfloat16 [16384, 1024], P(('dp', 'tensor')), may hold values from -6 to 6
Outputs:
- output: bfloat16 [16384, 1024], P(('dp', 'tensor'))
- grad_inputs: float32 [16384, 1024], P(('dp', 'tensor'))
- grad_attn_gain: float32 [1024], replicated
- grad_attn_bias: float32 [1024], replicated
- grad_mlp_gain: float32 [1024], replicated
- grad_mlp_bias: float32 [1024], replicated
- grad_w_qkv: float32 [1024, 3072], P('dp', 'tensor')
- grad_b_qkv: float32 [3072], P('tensor')
- grad_w_out: float32 [1024, 1024], P('tensor', 'dp')
- grad_b_out: float32 [1024], replicated
- grad_w_up: float32 [1024, 4096], P('dp', 'tensor')
- grad_b_up: float32 [4096], P('tensor')
- grad_w_down: float32 [4096, 1024], P('tensor', 'dp')
- grad_b_down: float32 [1024], replicated
The draws below stay inside these ranges and needn't reach their ends.
All inputs are finite; a program needn't handle non-finite values.
Results may differ from the reference program's by a relative error of at most 0.012.
Values may be sent and summed in bfloat16 or wider, within the bound.
No kernel may reach another device: no remote copies, remote signals or barrier semaphores. Data moves between devices by JAX's collectives and lax.ppermute only.
A program may use at most 192 MiB of HBM per device.

```python
import math
import jax
import jax.numpy as jnp
from jax import lax

D = 1024
H = 16
HD = 64
FF = 4096
ROT = 16
SEQ = 1024
TOKENS = 16384


def spiked(array, own_key, source, target, blocks, factor):
    def block_of(axis_at):
        return (jnp.arange(array.shape[axis_at]) // (array.shape[axis_at] // blocks)).reshape((-1,) + (1,) * (array.ndim - 1 - axis_at))

    one_side = jax.random.permutation(own_key, blocks)[block_of(target)]
    other_side = (block_of(target) + blocks // 2) % blocks
    return jnp.where((block_of(source) == one_side) | (block_of(source) == other_side), factor * array, array)


def block_scale(rng, dims, split, least, top_value):
    level, own = 1.0, jax.random.fold_in(rng, 6)
    for position, blocks in split:
        heights = jnp.exp(jax.random.uniform(jax.random.fold_in(own, position), (blocks,), jnp.float32, least / len(split), top_value / len(split)))
        level = level * jnp.repeat(heights, dims[position] // blocks).reshape([-1 if axis == position else 1 for axis in range(len(dims))])
    return level


def noise(key, dims, deviation, bound, split=(), kind=jnp.bfloat16):
    values = jax.random.normal(key, dims, jnp.float32) * deviation
    if len(split) > 0:
        values = block_scale(key, dims, split, -0.22, 0.18) * values
    return jnp.clip(values, min=-bound, max=bound).astype(kind)


def heavy_noise(own_key, dims, scale, limit, split, heavy, held_as=jnp.bfloat16):
    values = scale * jax.random.normal(own_key, dims, jnp.float32)
    if split:
        values = values * block_scale(own_key, dims, split, -0.22, 0.18)
    return jnp.clip(spiked(values, jax.random.fold_in(own_key, 3), *heavy), -limit, limit).astype(held_as)


def setup_inputs(seed: int = 0) -> dict:
    streams_of = jax.random.split(jax.random.key(seed), 15)
    inputs = noise(streams_of[0], (TOKENS, D), 1.0, 6.0, ((0, 32),))
    attn_gain = jnp.clip(1.0 + 0.15 * jax.random.normal(streams_of[1], (D,), jnp.float32), 0.25, 1.75)
    attn_bias = noise(streams_of[2], (D,), 0.3, 4.0, (), jnp.float32)
    mlp_gain = jnp.clip(1.0 + 0.15 * jax.random.normal(streams_of[3], (D,), jnp.float32), 0.25, 1.75)
    mlp_bias = noise(streams_of[4], (D,), 0.3, 4.0, (), jnp.float32)
    w_qkv = noise(streams_of[5], (D, 3 * D), D ** -0.5, 0.1875, ((0, 16), (1, 2)))
    b_qkv = noise(streams_of[6], (3 * D,), 0.3, 4.0, ((0, 2),), jnp.float32)
    w_out = noise(streams_of[7], (D, D), (max(1, D * 8 // SEQ)) ** -0.5, 2.0, ((0, 2), (1, 16)))
    b_out = noise(streams_of[8], (D,), 0.3, 4.0, (), jnp.float32)
    w_up = noise(streams_of[9], (D, FF), D ** -0.5, 0.1875, ((0, 16), (1, 2)))
    b_up = noise(streams_of[10], (FF,), 0.3, 4.0, ((0, 2),), jnp.float32)
    w_down = noise(streams_of[11], (FF, D), FF ** -0.5, 0.09375, ((0, 2), (1, 16)))
    b_down = noise(streams_of[12], (D,), 0.3, 4.0, (), jnp.float32)
    cotangent = heavy_noise(streams_of[13], (TOKENS, D), 1.0, 6.0, ((0, 32),), (0, 1, 32, 2.75))
    return {"inputs": inputs, "attn_gain": attn_gain, "attn_bias": attn_bias, "mlp_gain": mlp_gain, "mlp_bias": mlp_bias, "w_qkv": w_qkv, "b_qkv": b_qkv, "w_out": w_out, "b_out": b_out, "w_up": w_up, "b_up": b_up, "w_down": w_down, "b_down": b_down, "cotangent": cotangent}


@jax.custom_vjp
def low(v):
    return lax.optimization_barrier(v.astype(jnp.bfloat16)).astype(jnp.float32)

@jax.custom_vjp
def low_back(v):
    return v

def low_keep(v):
    return (low(v), None)

def low_pass(kept, grad):
    return (grad,)

def back_keep(v):
    return (v, None)

def back_low(kept, grad):
    return (low(grad),)
low.defvjp(low_keep, low_pass)
low_back.defvjp(back_keep, back_low)
EPSILON = 1e-05
HIGHEST = lax.Precision.HIGHEST

def layer_norm(rows, gain, bias):
    average = lax.optimization_barrier(jnp.mean(rows, axis=-1, keepdims=True))
    centered = rows - average
    spread = lax.optimization_barrier(jnp.mean(centered * centered, axis=-1, keepdims=True))
    return centered * lax.rsqrt(spread + EPSILON) * gain + bias

def rotary(entries, angles):
    half_rot = angles.shape[-1]
    cosine = jnp.cos(angles)[:, None, :]
    sine_part = jnp.sin(angles)[:, None, :]
    leading = entries[..., :half_rot]
    trailing = entries[..., half_rot:2 * half_rot]
    return jnp.concatenate([leading * cosine - trailing * sine_part, trailing * cosine + leading * sine_part, entries[..., 2 * half_rot:]], axis=-1)

def rotary_angles(count):
    positions = (jnp.arange(count, dtype=jnp.int32) % SEQ).astype(jnp.float32)
    inverse = 10000.0 ** (-(2.0 * jnp.arange(ROT // 2, dtype=jnp.float32)) / ROT)
    return positions[:, None] * inverse[None, :]

def attend(queries, keys, values):
    block = min(512, SEQ)
    count = SEQ // block
    scale = 1.0 / math.sqrt(HD)

    def one_block(index):
        start = (index * block).astype(jnp.int32)
        query_rows = lax.dynamic_slice_in_dim(queries, start, block, 0)
        scores = jnp.einsum('qhd,khd->hqk', query_rows, keys, precision=HIGHEST) * scale
        scores = low_back(scores)
        query_pos = start + jnp.arange(block, dtype=jnp.int32)
        key_pos = jnp.arange(SEQ, dtype=jnp.int32)
        allowed = (key_pos[None, :] <= query_pos[:, None])[None]
        scores = jnp.where(allowed, scores, -1e+30)
        highest = lax.optimization_barrier(jnp.max(scores, axis=-1, keepdims=True))
        expos = jnp.exp(scores - highest)
        probs = expos / lax.optimization_barrier(jnp.sum(expos, axis=-1, keepdims=True))
        probs_low = low(probs)
        return jnp.einsum('hqk,khd->qhd', probs_low, values, precision=HIGHEST)
    blocks = lax.map(jax.checkpoint(one_block), jnp.arange(count, dtype=jnp.int32))
    return blocks.reshape(SEQ, H, HD)

def sequence_block(params, rows):
    attn_gain, attn_bias, mlp_gain, mlp_bias, w_qkv, b_qkv, w_out, b_out, w_up, b_up, w_down, b_down = params
    normed_one = low(layer_norm(rows, attn_gain, attn_bias))
    normed_two = low(layer_norm(rows, mlp_gain, mlp_bias))
    mixed = low_back(jnp.dot(normed_one, w_qkv, precision=HIGHEST, preferred_element_type=jnp.float32) + b_qkv)
    mixed = mixed.reshape(SEQ, H, 3, HD)
    angles = rotary_angles(SEQ)
    queries = low(rotary(mixed[:, :, 0], angles))
    keys = low(rotary(mixed[:, :, 1], angles))
    values = low(mixed[:, :, 2])
    context = low_back(low(attend(queries, keys, values))).reshape(SEQ, D)
    hidden = low_back(jnp.dot(normed_two, w_up, precision=HIGHEST, preferred_element_type=jnp.float32) + b_up)
    active = low(jax.nn.gelu(hidden, approximate=False))
    branch = jnp.dot(context, w_out, precision=HIGHEST, preferred_element_type=jnp.float32) + jnp.dot(active, w_down, precision=HIGHEST, preferred_element_type=jnp.float32)
    return rows + branch + b_out + b_down

def reference(inputs, attn_gain, attn_bias, mlp_gain, mlp_bias, w_qkv, b_qkv, w_out, b_out, w_up, b_up, w_down, b_down, cotangent):
    params = tuple((p.astype(jnp.float32) for p in (attn_gain, attn_bias, mlp_gain, mlp_bias, w_qkv, b_qkv, w_out, b_out, w_up, b_up, w_down, b_down)))
    count = TOKENS // SEQ
    seq_rows = inputs.astype(jnp.float32).reshape(count, SEQ, D)
    seq_grads = cotangent.astype(jnp.float32).reshape(count, SEQ, D)
    zeros = jax.tree.map(jnp.zeros_like, params)

    def step(totals, pair):
        rows, grad_out = pair
        result, pullback = jax.vjp(sequence_block, params, rows)
        grad_params, grad_rows = pullback(grad_out)
        return (jax.tree.map(jnp.add, totals, grad_params), (result.astype(jnp.bfloat16), grad_rows))
    totals, (results, grad_rows) = lax.scan(step, zeros, (seq_rows, seq_grads))
    g_attn_gain, g_attn_bias, g_mlp_gain, g_mlp_bias, g_w_qkv, g_b_qkv, g_w_out, g_b_out, g_w_up, g_b_up, g_w_down, g_b_down = totals
    return (results.reshape(TOKENS, D), grad_rows.reshape(TOKENS, D), g_attn_gain, g_attn_bias, g_mlp_gain, g_mlp_bias, g_w_qkv, g_b_qkv, g_w_out, g_b_out, g_w_up, g_b_up, g_w_down, g_b_down)
```

```python
import jax
import jax.numpy as jnp
import numpy as np
from jax import lax
from jax.experimental import pallas as pl
from jax.experimental.pallas import tpu as pltpu
from jax.sharding import PartitionSpec as P

HD = 64
ROT = 16
SEQ = 1024
EPSILON = 1e-05
PAIR = 2 * HD
TRIPLE = 6 * HD
BOTH = TRIPLE + PAIR
Q_BLOCK = 256
ROW_BLOCK = 256
UNIT_BLOCK = 512
VMEM_BYTES = 60 * 1024 * 1024
F32 = jnp.float32
BF16 = jnp.bfloat16
ANY = pl.BlockSpec(memory_space=pl.ANY)


def normalize(rows):
    average = jnp.mean(rows, axis=-1, keepdims=True)
    centered = rows - average
    spread = jnp.mean(centered * centered, axis=-1, keepdims=True)
    rate = lax.rsqrt(spread + EPSILON)
    return centered * rate, rate


def rotary_tables(count):
    positions = (np.arange(count) % SEQ).astype(np.float32)
    inverse = (10000.0 ** (-(2.0 * np.arange(ROT // 2)) / ROT)).astype(np.float32)
    angles = (positions[:, None] * inverse[None, :]).astype(np.float64)
    cosine, sine = np.cos(angles), np.sin(angles)
    none = np.zeros_like(sine)
    rest = np.zeros((count, HD - ROT))
    keep = np.concatenate([cosine, cosine, rest + 1.0], axis=1)
    down = np.concatenate([none, sine, rest], axis=1)
    up = np.concatenate([-sine, none, rest], axis=1)
    return tuple(jnp.asarray(np.concatenate([t, t], axis=1), F32) for t in (keep, down, up))


def nn(left, right):
    return jnp.dot(left, right, preferred_element_type=F32)


def nt(left, right):
    return lax.dot_general(left, right, (((1,), (1,)), ((), ())), preferred_element_type=F32)


def place_rows(order, which, parts, target):
    count, rows, _ = parts[0].shape
    for index, part in enumerate(parts):
        for slot in range(count):
            at = pl.multiple_of(order[which, index * count + slot] * rows, rows)
            target[pl.ds(at, rows), :] = part[slot]


def split_rows(order, which, source, parts):
    count, rows, _ = parts[0].shape
    for index, part in enumerate(parts):
        for slot in range(count):
            at = pl.multiple_of(order[which, index * count + slot] * rows, rows)
            part[slot] = source[pl.ds(at, rows), :]


def whole(shape):
    return pl.BlockSpec(shape, lambda i, *_: (0,) * len(shape))


def once(shape):
    return pl.BlockSpec(shape, lambda i, *_: (0,) * len(shape), pipeline_mode=pl.Buffered(1))


def shape_of(shape, dtype):
    return jax.ShapeDtypeStruct(shape, dtype)


def norm_kernel(place, own, other, gains, normed_one, normed_two, one_t, two_t, hat):
    mine = pl.program_id(0) // (pl.num_programs(0) // 2) == place[0]
    rows = jnp.where(mine, own[...], other[...]).astype(F32)
    xhat, _ = normalize(rows)
    one = (xhat * gains[0:1, :] + gains[1:2, :]).astype(BF16)
    two = (xhat * gains[2:3, :] + gains[3:4, :]).astype(BF16)
    normed_one[...] = one
    normed_two[...] = two
    one_t[...] = one.T
    two_t[...] = two.T
    hat[...] = xhat.astype(BF16)


def turn_kernel(place, own, other, rows_out, turned):
    mine = pl.program_id(0) // (pl.num_programs(0) // 2) == place[0]
    rows = jnp.where(mine, own[...], other[...])
    rows_out[...] = rows
    turned[...] = rows.T


def two_sided(kernel, place, own, other, extra, straight, flipped):
    rows, width = own.shape
    steps = 2 * rows // ROW_BLOCK
    half = pl.BlockSpec((ROW_BLOCK, width), lambda i, *_: (i % (steps // 2), 0))
    row_spec = pl.BlockSpec((ROW_BLOCK, width), lambda i, *_: (i, 0))
    col_spec = pl.BlockSpec((width, ROW_BLOCK), lambda i, *_: (0, i))
    before, after = straight
    return pl.pallas_call(
        kernel,
        grid_spec=pltpu.PrefetchScalarGridSpec(
            num_scalar_prefetch=1,
            grid=(steps,),
            in_specs=[half, half] + [whole(e.shape) for e in extra],
            out_specs=[row_spec] * before + [col_spec] * flipped + [row_spec] * after,
        ),
        out_shape=[shape_of((2 * rows, width), BF16)] * before
        + [shape_of((width, 2 * rows), BF16)] * flipped
        + [shape_of((2 * rows, width), BF16)] * after,
        compiler_params=pltpu.CompilerParams(vmem_limit_bytes=VMEM_BYTES),
        name=kernel.__name__,
    )(place, own, other, *extra)


def mlp_call(order, n2, n2t, dy, dyt, bias, parts, outs, init=None, final=None, after=()):
    tokens, width = n2.shape
    count, rows, both = parts[0].shape
    units = both // 2
    block = min(UNIT_BLOCK, units)
    steps = units // block
    n_parts = len(parts)
    slots = count * n_parts // outs

    def kernel(order, *refs):
        refs = list(refs)
        take = lambda n: [refs.pop(0) for _ in range(n)]
        n2, dy, n2t_hbm, dyt_hbm, bias = take(5)
        weights = take(n_parts)
        starts = take(2 if init is not None else 0)
        hat_hbm, gain = take(2) if final is not None else (None, None)
        take(len(after))
        grads = take(outs)
        gbias, branch, dnormed = take(3)
        sums = take(1)[0] if final is not None else None
        w, act, dhid, gwide, n2t, dyt, sem = take(7)
        hat = take(1)[0] if final is not None else None
        step = pl.program_id(0)
        loads = [
            pltpu.make_async_copy(n2t_hbm, n2t, sem.at[0]),
            pltpu.make_async_copy(dyt_hbm, dyt, sem.at[1]),
        ]
        if init is not None:
            inits = [
                pltpu.make_async_copy(starts[0], branch, sem.at[2]),
                pltpu.make_async_copy(starts[1], dnormed, sem.at[3]),
            ]
        if final is not None:
            loads.append(pltpu.make_async_copy(hat_hbm, hat, sem.at[4]))

        @pl.when(step == 0)
        def _():
            if init is not None:
                for copy in inits:
                    copy.start()
            else:
                branch[...] = jnp.zeros_like(branch)
                dnormed[...] = jnp.zeros_like(dnormed)
            for copy in loads:
                copy.start()

        place_rows(order, 0, weights, w)
        total = jnp.zeros((1, block), F32)
        for start in range(0, tokens, ROW_BLOCK):
            at = slice(start, start + ROW_BLOCK)
            hidden = nn(n2[at, :], w[:, :block]) + bias[...]
            dactive = nn(dy[at, :], w[:, block:])
            below = 0.5 + 0.5 * lax.erf(hidden * 0.7071067811865476)
            density = jnp.exp(hidden * hidden * -0.5) * 0.3989422804014327
            dhidden = (dactive * (below + hidden * density)).astype(BF16)
            act[at, :] = (hidden * below).astype(BF16)
            dhid[at, :] = dhidden
            total += jnp.sum(dhidden.astype(F32), axis=0, keepdims=True)
        gbias[...] = total

        @pl.when(step == 0)
        def _():
            if init is not None:
                for copy in inits:
                    copy.wait()
            for copy in loads:
                copy.wait()

        for start in range(0, tokens, ROW_BLOCK):
            at = slice(start, start + ROW_BLOCK)
            branch[at, :] += nt(act[at, :], w[:, block:])
            dnormed[at, :] += nt(dhid[at, :], w[:, :block])
        gwide[:, :block] = nn(n2t[...], dhid[...]).astype(BF16)
        gwide[:, block:] = nn(dyt[...], act[...]).astype(BF16)
        split_rows(order, 1, gwide, grads)
        if final is not None:

            @pl.when(step == steps - 1)
            def _():
                direct = dnormed[...]
                sums[0:1, :] = jnp.sum(direct * hat[...].astype(F32), axis=0, keepdims=True)
                sums[1:2, :] = jnp.sum(direct, axis=0, keepdims=True)
                dnormed[...] = direct * gain[...]

    part_spec = pl.BlockSpec((count, rows, 2 * block), lambda i, *_: (0, 0, i))
    grad_spec = pl.BlockSpec((slots, rows, 2 * block), lambda i, *_: (0, 0, i))
    bias_spec = pl.BlockSpec((1, block), lambda i, *_: (0, i))
    square = (tokens, width)
    in_specs = [once(square), once(square), ANY, ANY, bias_spec] + [part_spec] * n_parts
    operands = [n2, dy, n2t, dyt, bias, *parts]
    out_specs = [grad_spec] * outs + [bias_spec, whole(square), whole(square)]
    out_shape = [shape_of((slots, rows, both), BF16)] * outs + [
        shape_of((1, units), F32), shape_of(square, F32), shape_of(square, F32),
    ]
    scratch = [
        pltpu.VMEM((width, 2 * block), BF16), pltpu.VMEM((tokens, block), BF16), pltpu.VMEM((tokens, block), BF16),
        pltpu.VMEM((width, 2 * block), BF16), pltpu.VMEM((width, tokens), BF16), pltpu.VMEM((width, tokens), BF16),
        pltpu.SemaphoreType.DMA((5,)),
    ]
    if init is not None:
        in_specs += [ANY, ANY]
        operands += list(init)
    if final is not None:
        hat, gain = final
        in_specs += [ANY, whole((1, width))]
        operands += [hat, gain[None]]
        out_specs += [whole((2, width))]
        out_shape += [shape_of((2, width), F32)]
        scratch += [pltpu.VMEM(square, BF16)]
    in_specs += [ANY] * len(after)
    operands += list(after)
    return pl.pallas_call(
        kernel,
        grid_spec=pltpu.PrefetchScalarGridSpec(
            num_scalar_prefetch=1, grid=(steps,), in_specs=in_specs, out_specs=out_specs, scratch_shapes=scratch
        ),
        out_shape=out_shape,
        compiler_params=pltpu.CompilerParams(vmem_limit_bytes=VMEM_BYTES),
        cost_estimate=pl.CostEstimate(
            flops=12 * tokens * width * units, transcendentals=2 * tokens * units, bytes_accessed=32 * tokens * width
        ),
        name="mlp_both_ways",
    )(order, *operands)


def attention_call(order, n1, n1t, dy, dyt, tables, bias, parts, outs, first, pairs, init=None, final=None, after=()):
    tokens, width = n1.shape
    count, rows, _ = parts[0].shape
    n_parts = len(parts)
    slots = count * n_parts // outs
    home_rows = final[3] if final is not None else 0
    half = ROT // 2

    def kernel(order, *refs):
        refs = list(refs)
        take = lambda n: [refs.pop(0) for _ in range(n)]
        n1, dy, n1t_hbm, dyt_hbm, keep, down, up, bias = take(8)
        weights = take(n_parts)
        starts = take(2 if init is not None else 0)
        share_hbm, hat_hbm, gain = take(3) if final is not None else (None, None, None)
        take(len(after))
        grads = take(outs)
        (gbias,) = take(1)
        if final is None:
            branch, dnormed = take(2)
        else:
            sums, branch_home, branch_away, share_home, share_away = take(5)
        w, turned, dctx, ctx_t, dq_t, dk, dv, gwide, n1t, dyt, sem = take(11)
        if final is not None:
            branch, dnormed, share, hat = take(4)
        step = pl.program_id(0)
        loads = [
            pltpu.make_async_copy(n1t_hbm, n1t, sem.at[0]),
            pltpu.make_async_copy(dyt_hbm, dyt, sem.at[1]),
        ]
        if init is not None:
            loads.append(pltpu.make_async_copy(starts[0], branch, sem.at[2]))
            if len(starts) > 1:
                loads.append(pltpu.make_async_copy(starts[1], dnormed, sem.at[3]))
        if final is not None:
            loads.append(pltpu.make_async_copy(share_hbm, share, sem.at[4]))
            loads.append(pltpu.make_async_copy(hat_hbm, hat, sem.at[5]))

        @pl.when(step == 0)
        def _():
            for copy in loads:
                copy.start()
            if init is None:
                branch[...] = jnp.zeros_like(branch)
                dnormed[...] = jnp.zeros_like(dnormed)

        lane = lax.broadcasted_iota(jnp.int32, (tokens, PAIR), 1)

        def rotate(rows, sign):
            turns = [
                r * keep[...] + sign * (pltpu.roll(r, half, 1) * down[...] + pltpu.roll(r, PAIR - half, 1) * up[...])
                for r in rows
            ]
            return [turns[0], jnp.where(lane >= HD, turns[1], rows[1]), jnp.where(lane < HD, turns[2], rows[2])]

        place_rows(order, 0, weights, w)
        mixed = nn(n1[...], w[:, :TRIPLE]) + bias[...]
        for index, group in enumerate(rotate([mixed[:, i * PAIR : (i + 1) * PAIR] for i in range(3)], 1.0)):
            turned[:, index * PAIR : (index + 1) * PAIR] = group.astype(BF16)
        dctx[...] = nn(dy[...], w[:, TRIPLE:]).astype(BF16)
        behind = lax.broadcasted_iota(jnp.int32, (Q_BLOCK, Q_BLOCK), 0) > lax.broadcasted_iota(
            jnp.int32, (Q_BLOCK, Q_BLOCK), 1
        )
        pieces = []
        for head in range(2):
            base = head * 3 * HD
            query = turned[:, base : base + HD] * jnp.asarray(0.125, BF16)
            key = turned[:, base + HD : base + 2 * HD]
            value = turned[:, base + 2 * HD : base + 3 * HD]
            grad = dctx[:, head * HD : (head + 1) * HD]
            key_t = key.T
            value_t = value.T
            dk[...] = jnp.zeros_like(dk)
            dv[...] = jnp.zeros_like(dv)
            for start in range(0, tokens, Q_BLOCK):
                stop = start + Q_BLOCK
                query_rows = query[start:stop]
                grad_rows = grad[start:stop]
                scores = nt(key[:stop], query_rows)
                last = jnp.where(behind, -1e30, scores[start:])
                scores = last if start == 0 else jnp.concatenate([scores[:start], last], axis=0)
                expos = jnp.exp(scores - jnp.max(scores, axis=0, keepdims=True))
                probs = expos * (1.0 / jnp.sum(expos, axis=0, keepdims=True))
                low = probs.astype(BF16)
                dprobs = nt(value[:stop], grad_rows)
                inner = jnp.sum(probs * dprobs, axis=0, keepdims=True)
                dscores = (probs * (dprobs - inner)).astype(BF16)
                ctx_t[head * HD : (head + 1) * HD, start:stop] = nn(value_t[:, :stop], low)
                dq_t[head * HD : (head + 1) * HD, start:stop] = nn(key_t[:, :stop], dscores) * 0.125
                dk[:stop, :] += nn(dscores, query_rows)
                dv[:stop, :] += nn(low, grad_rows)
            pieces += [None, dk[...], dv[...]]
        dq = dq_t[...].T
        pieces[0], pieces[3] = dq[:, :HD], dq[:, HD:]
        groups = rotate([jnp.concatenate(pieces[2 * i : 2 * i + 2], axis=1) for i in range(3)], -1.0)
        dmixed = jnp.concatenate(groups, axis=1).astype(BF16)
        context = ctx_t[...].T.astype(BF16)
        gbias[...] = jnp.sum(dmixed.astype(F32), axis=0, keepdims=True)

        @pl.when(step == 0)
        def _():
            for copy in loads:
                copy.wait()

        dnormed[...] += nt(dmixed, w[:, :TRIPLE])
        branch[...] += nt(context, w[:, TRIPLE:])
        gwide[:, :TRIPLE] = nn(n1t[...], dmixed).astype(BF16)
        gwide[:, TRIPLE:] = nn(dyt[...], context).astype(BF16)
        split_rows(order, 1, gwide, grads)
        if final is not None:

            @pl.when(step == pairs - 1)
            def _():
                direct = dnormed[...]
                sums[0:1, :] = jnp.sum(direct * hat[...].astype(F32), axis=0, keepdims=True)
                sums[1:2, :] = jnp.sum(direct, axis=0, keepdims=True)
                dnormed[...] = direct * gain[...] + share[...]
                home = pl.multiple_of(order[2, 0] * home_rows, home_rows)
                away = pl.multiple_of(order[2, 1] * (tokens - home_rows), 8)
                share_home[...] = dnormed[pl.ds(home, home_rows), :]
                branch_home[...] = branch[pl.ds(home, home_rows), :]
                if home_rows < tokens:
                    share_away[...] = dnormed[pl.ds(away, tokens - home_rows), :].astype(BF16)
                    branch_away[...] = branch[pl.ds(away, tokens - home_rows), :].astype(BF16)

    part_spec = pl.BlockSpec((count, rows, BOTH), lambda i, *_: (0, 0, i + first))
    grad_spec = pl.BlockSpec((slots, rows, BOTH), lambda i, *_: (0, 0, i))
    square = (tokens, width)
    table = whole((tokens, PAIR))
    in_specs = [
        once(square), once(square), ANY, ANY, table, table, table,
        pl.BlockSpec((1, TRIPLE), lambda i, *_: (0, i + first)),
    ] + [part_spec] * n_parts
    operands = [n1, dy, n1t, dyt, *tables, bias, *parts]
    out_specs = [grad_spec] * outs + [pl.BlockSpec((1, TRIPLE), lambda i, *_: (0, i))]
    out_shape = [shape_of((slots, rows, BOTH * pairs), BF16)] * outs + [shape_of((1, TRIPLE * pairs), F32)]
    scratch = [
        pltpu.VMEM((width, BOTH), BF16), pltpu.VMEM((tokens, TRIPLE), BF16), pltpu.VMEM((tokens, PAIR), BF16),
        pltpu.VMEM((PAIR, tokens), F32), pltpu.VMEM((PAIR, tokens), F32),
        pltpu.VMEM((tokens, HD), F32), pltpu.VMEM((tokens, HD), F32),
        pltpu.VMEM((width, BOTH), BF16), pltpu.VMEM((width, tokens), BF16), pltpu.VMEM((width, tokens), BF16),
        pltpu.SemaphoreType.DMA((6,)),
    ]
    if init is not None:
        in_specs += [ANY] * 2
        operands += list(init)
    if final is None:
        out_specs += [whole(square), whole(square)]
        out_shape += [shape_of(square, F32), shape_of(square, F32)]
    else:
        share, hat, gain, _ = final
        in_specs += [ANY, ANY, whole((1, width))]
        operands += [share, hat, gain[None]]
        home, away = (home_rows, width), (max(tokens - home_rows, 16), width)
        out_specs += [whole((2, width)), whole(home), whole(away), whole(home), whole(away)]
        out_shape += [
            shape_of((2, width), F32), shape_of(home, F32), shape_of(away, BF16), shape_of(home, F32), shape_of(away, BF16),
        ]
        scratch += [pltpu.VMEM(square, F32), pltpu.VMEM(square, F32), pltpu.VMEM(square, F32), pltpu.VMEM(square, BF16)]
    in_specs += [ANY] * len(after)
    operands += list(after)
    return pl.pallas_call(
        kernel,
        grid_spec=pltpu.PrefetchScalarGridSpec(
            num_scalar_prefetch=1, grid=(pairs,), in_specs=in_specs, out_specs=out_specs, scratch_shapes=scratch
        ),
        out_shape=out_shape,
        compiler_params=pltpu.CompilerParams(vmem_limit_bytes=VMEM_BYTES),
        cost_estimate=pl.CostEstimate(
            flops=pairs * 20 * tokens * width * BOTH, transcendentals=pairs * tokens * tokens,
            bytes_accessed=32 * tokens * width,
        ),
        name="attention_both_ways",
    )(order, *operands)


def swap_dp(array, bits):
    count = lax.axis_size("dp")
    return lax.ppermute(array, "dp", [(i, i ^ bits) for i in range(count)])


def swap_tensor(array):
    return lax.ppermute(array, "tensor", [(0, 1), (1, 0)])


def near_order():
    count = lax.axis_size("dp")
    slots = np.arange(count)
    bits = (slots % 4) * 4 + (slots // 4 % 2) * 2 + slots // 8
    return jnp.asarray(bits, jnp.int32) ^ lax.axis_index("dp").astype(jnp.int32)


def gather_lines(piece):
    return jnp.concatenate([piece] + [swap_dp(piece, 4 * s) for s in (1, 2, 3)], axis=0)


def gather_plane(lines):
    return jnp.concatenate([lines, swap_dp(lines, 2)], axis=0)


def add_low(left, right):
    return (left.astype(F32) + right.astype(F32)).astype(BF16)


def sum_lines(lines):
    total = lines[0].astype(F32)
    for s in (1, 2, 3):
        total = total + swap_dp(lines[s], 4 * s).astype(F32)
    return total


def paired(one, other, size_one, size_other):
    steps = one.shape[1] // size_one
    return jnp.concatenate(
        [
            part
            for i in range(steps)
            for part in (one[:, i * size_one : (i + 1) * size_one], other[:, i * size_other : (i + 1) * size_other])
        ],
        axis=1,
    )


def unpaired(both, size_one, size_other):
    size = size_one + size_other
    steps = both.shape[1] // size
    one = jnp.concatenate([both[:, i * size : i * size + size_one] for i in range(steps)], axis=1)
    other = jnp.concatenate([both[:, i * size + size_one : (i + 1) * size] for i in range(steps)], axis=1)
    return one, other


def on_device(
    inputs, attn_gain, attn_bias, mlp_gain, mlp_bias, w_qkv, b_qkv, w_out, b_out, w_up, b_up, w_down, b_down, cotangent
):
    own_rows, width = inputs.shape
    units = w_up.shape[1]
    columns = w_qkv.shape[1]
    pairs = columns // TRIPLE
    piece_rows = w_up.shape[0]
    n_dp, n_tensor = lax.axis_size("dp"), lax.axis_size("tensor")
    by_hand = n_dp == 16 and n_tensor == 2
    block = min(UNIT_BLOCK, units)
    gains = jnp.stack([attn_gain, attn_bias, mlp_gain, mlp_bias])
    natural = jnp.arange(n_dp, dtype=jnp.int32)
    side = lax.axis_index("tensor").astype(jnp.int32)
    tables = rotary_tables(own_rows * n_tensor)

    def full_gather(piece):
        return lax.all_gather(piece, "dp", axis=0, tiled=True).reshape(n_dp, piece_rows, piece.shape[1])

    def full_scatter(parts):
        return lax.psum_scatter(parts.reshape(width, parts.shape[2]), "dp", scatter_dimension=0, tiled=True).astype(F32)

    mlp_piece = paired(w_up, w_down.T, block, block)
    attn_piece = paired(w_qkv, w_out.T, TRIPLE, PAIR)
    cotangent_sum = jnp.sum(cotangent.astype(F32), axis=0)

    if by_hand:
        sides = jnp.zeros((n_dp,), jnp.int32).at[0].set(side).at[1].set(1 - side)
        near = near_order()
        place = side[None]
        half = mlp_piece.shape[1] // 2
        attn_parts = [full_gather(attn_piece)]
        lines_a = gather_lines(mlp_piece[:, :half])
        lines_b = gather_lines(mlp_piece[:, half:])
        x_other = swap_tensor(inputs)
        dy_other = swap_tensor(cotangent)
        plane_a = gather_plane(lines_a)
        plane_b = gather_plane(lines_b)
        eight = (n_dp // 2, piece_rows, half)
        parts_a = [plane_a.reshape(eight), swap_dp(plane_a, 1).reshape(eight)]
        parts_b = [plane_b.reshape(eight), swap_dp(plane_b, 1).reshape(eight)]
        n1, n2, n1t, n2t, hat = two_sided(norm_kernel, place, inputs, x_other, [gains], (2, 1), 2)
        dy, dyt = two_sided(turn_kernel, place, cotangent, dy_other, [], (1, 0), 1)

        wide, gb_a, branch, dn2 = mlp_call(
            jnp.stack([near, natural]), n2, n2t, dy, dyt, b_up[None, : units // 2], parts_a, 1, after=[lines_b]
        )
        grad_a = full_scatter(wide)
        keep_b, send_b, gb_b, branch, share, sums_two = mlp_call(
            jnp.stack([near, near]), n2, n2t, dy, dyt, b_up[None, units // 2 :], parts_b, 2,
            init=(branch, dn2), final=(hat, mlp_gain),
        )
        plane = add_low(keep_b, swap_dp(send_b, 1))
        attn_order = jnp.stack([natural, near, sides])
        first = pairs // 2
        keep_c, send_c, gb_c, branch, dn1 = attention_call(
            attn_order, n1, n1t, dy, dyt, tables, b_qkv[None], attn_parts, 2, 0, first,
            init=(branch, jnp.zeros_like(branch)), after=[plane],
        )
        lines = add_low(plane[:4], swap_dp(plane[4:], 2))
        plane_c = add_low(keep_c, swap_dp(send_c, 1))
        keep_d, send_d, gb_d, sums_one, branch_home, branch_away, share_home, share_away = attention_call(
            attn_order, n1, n1t, dy, dyt, tables, b_qkv[None], attn_parts, 2, first, pairs - first,
            init=(branch, dn1), final=(share, hat, attn_gain, own_rows), after=[lines, plane_c],
        )
        share_other = swap_tensor(share_away)
        branch_other = swap_tensor(branch_away)
        plane_d = add_low(keep_d, swap_dp(send_d, 1))
        grad_b = sum_lines(lines)
        grad_c = sum_lines(add_low(plane_c[:4], swap_dp(plane_c[4:], 2)))
        grad_d = sum_lines(add_low(plane_d[:4], swap_dp(plane_d[4:], 2)))
        mlp_grad = jnp.concatenate([grad_a, grad_b], axis=1)
        attn_grad = jnp.concatenate([grad_c, grad_d], axis=1)
        own_branch = branch_home + branch_other.astype(F32)
        own_share = share_home + share_other.astype(F32)
        small = jnp.concatenate(
            [gb_c[0], gb_d[0], gb_a[0], gb_b[0], sums_one.reshape(-1), sums_two.reshape(-1), cotangent_sum]
        )
        for bits in (1, 2, 4, 8):
            small = small + swap_dp(small, bits)
        tail = small[columns + units :]
        tail = tail + swap_tensor(tail)
    else:
        order = jnp.stack([natural, natural, jnp.zeros_like(natural)])
        x = lax.all_gather(inputs, "tensor", axis=0, tiled=True)
        dy = lax.all_gather(cotangent, "tensor", axis=0, tiled=True)
        mlp_parts = [full_gather(mlp_piece)]
        attn_parts = [full_gather(attn_piece)]
        rows = x.shape[0]
        place = jnp.zeros((1,), jnp.int32)
        n1, n2, n1t, n2t, hat = two_sided(
            norm_kernel, place, x[: rows // 2], x[rows // 2 :], [gains], (2, 1), 2
        )
        dy, dyt = two_sided(turn_kernel, place, dy[: rows // 2], dy[rows // 2 :], [], (1, 0), 1)
        wide, gb_up, branch, share, sums_two = mlp_call(
            order[:2], n2, n2t, dy, dyt, b_up[None], mlp_parts, 1, final=(hat, mlp_gain)
        )
        narrow, gb_qkv, sums_one, branch, _, share, _ = attention_call(
            order, n1, n1t, dy, dyt, tables, b_qkv[None], attn_parts, 1, 0, pairs,
            init=(branch, jnp.zeros_like(branch)), final=(share, hat, attn_gain, rows),
        )
        mlp_grad = full_scatter(wide)
        attn_grad = full_scatter(narrow)
        own_branch = lax.psum_scatter(branch.astype(BF16), "tensor", scatter_dimension=0, tiled=True).astype(F32)
        own_share = lax.psum_scatter(share.astype(BF16), "tensor", scatter_dimension=0, tiled=True).astype(F32)
        small = lax.psum(jnp.concatenate([gb_qkv[0], gb_up[0]]), "dp")
        tail = lax.psum(
            jnp.concatenate([sums_one.reshape(-1), sums_two.reshape(-1), cotangent_sum]), ("dp", "tensor")
        )

    sums = tail.reshape(5, width)
    own_x = inputs.astype(F32)
    output = (own_x + own_branch + b_out + b_down).astype(BF16)
    own_hat, own_rate = normalize(own_x)
    lead = jnp.mean(own_share, axis=-1, keepdims=True)
    along = jnp.mean(own_share * own_hat, axis=-1, keepdims=True)
    grad_inputs = cotangent.astype(F32) + own_rate * (own_share - lead - own_hat * along)
    grad_up, grad_down_t = unpaired(mlp_grad, block, block)
    grad_qkv, grad_out_t = unpaired(attn_grad, TRIPLE, PAIR)
    return (
        output,
        grad_inputs,
        sums[0],
        sums[1],
        sums[2],
        sums[3],
        grad_qkv,
        small[:columns],
        grad_out_t.T,
        sums[4],
        grad_up,
        small[columns : columns + units],
        grad_down_t.T,
        sums[4],
    )


def solution(mesh):
    rows = P(("dp", "tensor"), None)
    return jax.shard_map(
        on_device,
        mesh=mesh,
        in_specs=(
            rows, P(), P(), P(), P(), P("dp", "tensor"), P("tensor"), P("tensor", "dp"), P(),
            P("dp", "tensor"), P("tensor"), P("tensor", "dp"), P(), rows,
        ),
        out_specs=(
            rows, rows, P(), P(), P(), P(), P("dp", "tensor"), P("tensor"), P("tensor", "dp"), P(),
            P("dp", "tensor"), P("tensor"), P("tensor", "dp"), P(),
        ),
        check_vma=False,
    )
```

```python
import jax
import jax.numpy as jnp
import numpy as np
from jax import lax
from jax.experimental import pallas as pl
from jax.experimental.pallas import tpu as pltpu
from jax.sharding import PartitionSpec as P

HD = 64
ROT = 16
SEQ = 1024
EPSILON = 1e-05
PAIR = 2 * HD
TRIPLE = 6 * HD
BOTH = TRIPLE + PAIR
Q_BLOCK = 256
ROW_BLOCK = 256
UNIT_BLOCK = 512
VMEM_BYTES = 60 * 1024 * 1024
F32 = jnp.float32
BF16 = jnp.bfloat16
ANY = pl.BlockSpec(memory_space=pl.ANY)


def normalize(rows):
    average = jnp.mean(rows, axis=-1, keepdims=True)
    centered = rows - average
    spread = jnp.mean(centered * centered, axis=-1, keepdims=True)
    rate = lax.rsqrt(spread + EPSILON)
    return centered * rate, rate


def rotary_tables(count):
    positions = (np.arange(count) % SEQ).astype(np.float32)
    inverse = (10000.0 ** (-(2.0 * np.arange(ROT // 2)) / ROT)).astype(np.float32)
    angles = (positions[:, None] * inverse[None, :]).astype(np.float64)
    cosine, sine = np.cos(angles), np.sin(angles)
    none = np.zeros_like(sine)
    rest = np.zeros((count, HD - ROT))
    keep = np.concatenate([cosine, cosine, rest + 1.0], axis=1)
    down = np.concatenate([none, sine, rest], axis=1)
    up = np.concatenate([-sine, none, rest], axis=1)
    return tuple(jnp.asarray(np.concatenate([t, t], axis=1), F32) for t in (keep, down, up))


def nn(left, right):
    return jnp.dot(left, right, preferred_element_type=F32)


def nt(left, right):
    return lax.dot_general(left, right, (((1,), (1,)), ((), ())), preferred_element_type=F32)


def place_rows(order, which, parts, target):
    at = 0
    for part in parts:
        count, rows, _ = part.shape
        for slot in range(count):
            target[pl.ds(pl.multiple_of(order[which, at + slot] * rows, rows), rows), :] = part[slot]
        at += count


def split_rows(order, which, source, parts):
    at = 0
    for part in parts:
        count, rows, _ = part.shape
        for slot in range(count):
            part[slot] = source[pl.ds(pl.multiple_of(order[which, at + slot] * rows, rows), rows), :]
        at += count


def whole(shape):
    return pl.BlockSpec(shape, lambda i, *_: (0,) * len(shape))


def once(shape):
    return pl.BlockSpec(shape, lambda i, *_: (0,) * len(shape), pipeline_mode=pl.Buffered(1))


def shape_of(shape, dtype):
    return jax.ShapeDtypeStruct(shape, dtype)


def norm_kernel(place, own, other, gains, normed_one, normed_two, one_t, two_t, hat):
    mine = pl.program_id(0) // (pl.num_programs(0) // 2) == place[0]
    rows = jnp.where(mine, own[...], other[...]).astype(F32)
    xhat, _ = normalize(rows)
    one = (xhat * gains[0:1, :] + gains[1:2, :]).astype(BF16)
    two = (xhat * gains[2:3, :] + gains[3:4, :]).astype(BF16)
    normed_one[...] = one
    normed_two[...] = two
    one_t[...] = one.T
    two_t[...] = two.T
    hat[...] = xhat.astype(BF16)


def turn_kernel(place, own, other, rows_out, turned, total):
    mine = pl.program_id(0) // (pl.num_programs(0) // 2) == place[0]
    rows = jnp.where(mine, own[...], other[...])
    rows_out[...] = rows
    turned[...] = rows.T

    @pl.when(pl.program_id(0) == 0)
    def _():
        total[...] = jnp.zeros_like(total)

    @pl.when(mine)
    def _():
        total[...] += jnp.sum(own[...].astype(F32), axis=0, keepdims=True)


def two_sided(kernel, place, own, other, extra, straight, flipped, summed=0):
    rows, width = own.shape
    steps = 2 * rows // ROW_BLOCK
    half = pl.BlockSpec((ROW_BLOCK, width), lambda i, *_: (i % (steps // 2), 0))
    row_spec = pl.BlockSpec((ROW_BLOCK, width), lambda i, *_: (i, 0))
    col_spec = pl.BlockSpec((width, ROW_BLOCK), lambda i, *_: (0, i))
    before, after = straight
    return pl.pallas_call(
        kernel,
        grid_spec=pltpu.PrefetchScalarGridSpec(
            num_scalar_prefetch=1,
            grid=(steps,),
            in_specs=[half, half] + [whole(e.shape) for e in extra],
            out_specs=[row_spec] * before + [col_spec] * flipped + [row_spec] * after + [whole((1, width))] * summed,
        ),
        out_shape=[shape_of((2 * rows, width), BF16)] * before
        + [shape_of((width, 2 * rows), BF16)] * flipped
        + [shape_of((2 * rows, width), BF16)] * after
        + [shape_of((1, width), F32)] * summed,
        compiler_params=pltpu.CompilerParams(vmem_limit_bytes=VMEM_BYTES),
        name=kernel.__name__,
    )(place, own, other, *extra)


def mlp_call(order, n2, n2t, dy, dyt, bias, parts, chunk=(0, 1), buffer=None, init=None, final=None, after=()):
    tokens, width = n2.shape
    _, rows, both = parts[0].shape
    units = both // 2
    block = min(UNIT_BLOCK, units)
    steps = units // block
    n_parts = len(parts)
    slots = sum(part.shape[0] for part in parts)

    def kernel(order, *refs):
        refs = list(refs)
        take = lambda n: [refs.pop(0) for _ in range(n)]
        take(0 if buffer is None else 1)
        n2, dy, n2t_hbm, dyt_hbm, bias = take(5)
        weights = take(n_parts)
        starts = take(2 if init is not None else 0)
        hat_hbm, gain = take(2) if final is not None else (None, None)
        take(len(after))
        grads = take(1)
        gbias, branch, dnormed = take(3)
        sums = take(1)[0] if final is not None else None
        w, act, dhid, gwide, n2t, dyt, sem = take(7)
        hat = take(1)[0] if final is not None else None
        step = pl.program_id(0)
        loads = [
            pltpu.make_async_copy(n2t_hbm, n2t, sem.at[0]),
            pltpu.make_async_copy(dyt_hbm, dyt, sem.at[1]),
        ]
        if init is not None:
            inits = [
                pltpu.make_async_copy(starts[0], branch, sem.at[2]),
                pltpu.make_async_copy(starts[1], dnormed, sem.at[3]),
            ]
        if final is not None:
            loads.append(pltpu.make_async_copy(hat_hbm, hat, sem.at[4]))

        @pl.when(step == 0)
        def _():
            if init is not None:
                for copy in inits:
                    copy.start()
            else:
                branch[...] = jnp.zeros_like(branch)
                dnormed[...] = jnp.zeros_like(dnormed)
            for copy in loads:
                copy.start()

        place_rows(order, 0, weights, w)
        total = jnp.zeros((1, block), F32)
        for start in range(0, tokens, ROW_BLOCK):
            at = slice(start, start + ROW_BLOCK)
            hidden = nn(n2[at, :], w[:, :block]) + bias[...]
            dactive = nn(dy[at, :], w[:, block:])
            below = 0.5 + 0.5 * lax.erf(hidden * 0.7071067811865476)
            density = jnp.exp(hidden * hidden * -0.5) * 0.3989422804014327
            dhidden = (dactive * (below + hidden * density)).astype(BF16)
            act[at, :] = (hidden * below).astype(BF16)
            dhid[at, :] = dhidden
            total += jnp.sum(dhidden.astype(F32), axis=0, keepdims=True)
        gbias[...] = total

        @pl.when(step == 0)
        def _():
            if init is not None:
                for copy in inits:
                    copy.wait()
            for copy in loads:
                copy.wait()

        for start in range(0, tokens, ROW_BLOCK):
            at = slice(start, start + ROW_BLOCK)
            branch[at, :] += nt(act[at, :], w[:, block:])
            dnormed[at, :] += nt(dhid[at, :], w[:, :block])
        gwide[:, :block] = nn(n2t[...], dhid[...]).astype(BF16)
        gwide[:, block:] = nn(dyt[...], act[...]).astype(BF16)
        split_rows(order, 1, gwide, grads)
        if final is not None:

            @pl.when(step == steps - 1)
            def _():
                direct = dnormed[...]
                sums[0:1, :] = jnp.sum(direct * hat[...].astype(F32), axis=0, keepdims=True)
                sums[1:2, :] = jnp.sum(direct, axis=0, keepdims=True)
                dnormed[...] = direct * gain[...]

    part_specs = [pl.BlockSpec((part.shape[0], rows, 2 * block), lambda i, *_: (0, 0, i)) for part in parts]
    grad_spec = pl.BlockSpec((slots, rows, 2 * block), lambda i, *_: (0, 0, i + chunk[0] * steps))
    bias_spec = pl.BlockSpec((1, block), lambda i, *_: (0, i))
    square = (tokens, width)
    in_specs = [once(square), once(square), ANY, ANY, bias_spec] + part_specs
    operands = [n2, dy, n2t, dyt, bias, *parts]
    out_specs = [grad_spec, bias_spec, whole(square), whole(square)]
    out_shape = [
        shape_of((slots, rows, both * chunk[1]), BF16),
        shape_of((1, units), F32), shape_of(square, F32), shape_of(square, F32),
    ]
    if buffer is not None:
        in_specs = [ANY] + in_specs
        operands = [buffer] + operands
    scratch = [
        pltpu.VMEM((width, 2 * block), BF16), pltpu.VMEM((tokens, block), BF16), pltpu.VMEM((tokens, block), BF16),
        pltpu.VMEM((width, 2 * block), BF16), pltpu.VMEM((width, tokens), BF16), pltpu.VMEM((width, tokens), BF16),
        pltpu.SemaphoreType.DMA((5,)),
    ]
    if init is not None:
        in_specs += [ANY, ANY]
        operands += list(init)
    if final is not None:
        hat, gain = final
        in_specs += [ANY, whole((1, width))]
        operands += [hat, gain[None]]
        out_specs += [whole((2, width))]
        out_shape += [shape_of((2, width), F32)]
        scratch += [pltpu.VMEM(square, BF16)]
    in_specs += [ANY] * len(after)
    operands += list(after)
    return pl.pallas_call(
        kernel,
        grid_spec=pltpu.PrefetchScalarGridSpec(
            num_scalar_prefetch=1, grid=(steps,), in_specs=in_specs, out_specs=out_specs, scratch_shapes=scratch
        ),
        out_shape=out_shape,
        input_output_aliases={} if buffer is None else {1: 0},
        compiler_params=pltpu.CompilerParams(vmem_limit_bytes=VMEM_BYTES),
        cost_estimate=pl.CostEstimate(
            flops=12 * tokens * width * units, transcendentals=2 * tokens * units, bytes_accessed=32 * tokens * width
        ),
        name="mlp_both_ways",
    )(order, *operands)


def attention_call(order, n1, n1t, dy, dyt, tables, bias, parts, outs, first, pairs, init, home_rows, final=None, after=()):
    tokens, width = n1.shape
    rows = parts[0].shape[1]
    n_parts = len(parts)
    slots = sum(part.shape[0] for part in parts) // outs
    half = ROT // 2
    away_rows = tokens - home_rows
    last = final is not None
    shared = away_rows > 0
    early_rows = away_rows * 3 // 4

    def kernel(order, *refs):
        refs = list(refs)
        take = lambda n: [refs.pop(0) for _ in range(n)]
        n1, dy, n1t_hbm, dyt_hbm, keep, down, up, bias = take(8)
        weights = take(n_parts)
        starts = take(len(init))
        share_hbm, hat_hbm, gain = take(3) if final is not None else (None, None, None)
        take(len(after))
        grads = take(outs)
        (gbias,) = take(1)
        if last:
            sums, branch, share_home = take(3)
            share_first, share_second, ctx_away = take(3) if shared else (None, None, None)
        else:
            dnormed, branch_home, branch_away = take(3)
        w, turned, dctx, ctx_t, dq_t, dk, dv, gwide, n1t, dyt, sem = take(11)
        if last:
            dnormed, share, hat, ctx_rows = take(4)
        else:
            (branch,) = take(1)
        home = pl.multiple_of(order[2, 0] * home_rows, home_rows)
        away = pl.multiple_of(order[2, 1] * away_rows, 16)
        step = pl.program_id(0)
        loads = [
            pltpu.make_async_copy(n1t_hbm, n1t, sem.at[0]),
            pltpu.make_async_copy(dyt_hbm, dyt, sem.at[1]),
        ]
        for index, (start, total) in enumerate(zip(starts, (branch, dnormed))):
            loads.append(pltpu.make_async_copy(start, total, sem.at[2 + index]))
        if final is not None:
            loads.append(pltpu.make_async_copy(share_hbm, share, sem.at[4]))
            loads.append(pltpu.make_async_copy(hat_hbm, hat, sem.at[5]))

        @pl.when(step == 0)
        def _():
            for copy in loads:
                copy.start()
            for total in (branch, dnormed)[len(init) :]:
                total[...] = jnp.zeros_like(total)

        lane = lax.broadcasted_iota(jnp.int32, (tokens, PAIR), 1)

        def rotate(rows, sign):
            turns = [
                r * keep[...] + sign * (pltpu.roll(r, half, 1) * down[...] + pltpu.roll(r, PAIR - half, 1) * up[...])
                for r in rows
            ]
            return [turns[0], jnp.where(lane >= HD, turns[1], rows[1]), jnp.where(lane < HD, turns[2], rows[2])]

        place_rows(order, 0, weights, w)
        mixed = nn(n1[...], w[:, :TRIPLE]) + bias[...]
        for index, group in enumerate(rotate([mixed[:, i * PAIR : (i + 1) * PAIR] for i in range(3)], 1.0)):
            turned[:, index * PAIR : (index + 1) * PAIR] = group.astype(BF16)
        dctx[...] = nn(dy[...], w[:, TRIPLE:]).astype(BF16)
        behind = lax.broadcasted_iota(jnp.int32, (Q_BLOCK, Q_BLOCK), 0) > lax.broadcasted_iota(
            jnp.int32, (Q_BLOCK, Q_BLOCK), 1
        )
        pieces = []
        for head in range(2):
            base = head * 3 * HD
            query = turned[:, base : base + HD] * jnp.asarray(0.125, BF16)
            key = turned[:, base + HD : base + 2 * HD]
            value = turned[:, base + 2 * HD : base + 3 * HD]
            grad = dctx[:, head * HD : (head + 1) * HD]
            key_t = key.T
            value_t = value.T
            dk[...] = jnp.zeros_like(dk)
            dv[...] = jnp.zeros_like(dv)
            for start in range(0, tokens, Q_BLOCK):
                stop = start + Q_BLOCK
                query_rows = query[start:stop]
                grad_rows = grad[start:stop]
                scores = nt(key[:stop], query_rows)
                edge = jnp.where(behind, -1e30, scores[start:])
                scores = edge if start == 0 else jnp.concatenate([scores[:start], edge], axis=0)
                expos = jnp.exp(scores - jnp.max(scores, axis=0, keepdims=True))
                probs = expos * (1.0 / jnp.sum(expos, axis=0, keepdims=True))
                low = probs.astype(BF16)
                dprobs = nt(value[:stop], grad_rows)
                inner = jnp.sum(probs * dprobs, axis=0, keepdims=True)
                dscores = (probs * (dprobs - inner)).astype(BF16)
                ctx_t[head * HD : (head + 1) * HD, start:stop] = nn(value_t[:, :stop], low)
                dq_t[head * HD : (head + 1) * HD, start:stop] = nn(key_t[:, :stop], dscores) * 0.125
                dk[:stop, :] += nn(dscores, query_rows)
                dv[:stop, :] += nn(low, grad_rows)
            pieces += [None, dk[...], dv[...]]
        dq = dq_t[...].T
        pieces[0], pieces[3] = dq[:, :HD], dq[:, HD:]
        groups = rotate([jnp.concatenate(pieces[2 * i : 2 * i + 2], axis=1) for i in range(3)], -1.0)
        dmixed = jnp.concatenate(groups, axis=1).astype(BF16)
        context = ctx_t[...].T.astype(BF16)
        gbias[...] = jnp.sum(dmixed.astype(F32), axis=0, keepdims=True)

        @pl.when(step == 0)
        def _():
            for copy in loads:
                copy.wait()

        dnormed[...] += nt(dmixed, w[:, :TRIPLE])
        if last and shared:
            ctx_rows[...] = context
            ctx_away[...] = ctx_rows[pl.ds(away, away_rows), :]
            branch[...] += nt(ctx_rows[pl.ds(home, home_rows), :], w[:, TRIPLE:])
        else:
            branch[...] += nt(context, w[:, TRIPLE:])
        gwide[:, :TRIPLE] = nn(n1t[...], dmixed).astype(BF16)
        gwide[:, TRIPLE:] = nn(dyt[...], context).astype(BF16)
        split_rows(order, 1, gwide, grads)

        @pl.when(step == pairs - 1)
        def _():
            if last:
                direct = dnormed[...]
                sums[0:1, :] = jnp.sum(direct * hat[...].astype(F32), axis=0, keepdims=True)
                sums[1:2, :] = jnp.sum(direct, axis=0, keepdims=True)
                dnormed[...] = direct * gain[...] + share[...]
                share_home[...] = dnormed[pl.ds(home, home_rows), :]
                if shared:
                    share_first[...] = dnormed[pl.ds(away, early_rows), :].astype(BF16)
                    share_second[...] = dnormed[pl.ds(away + early_rows, away_rows - early_rows), :].astype(BF16)
            else:
                branch_home[...] = branch[pl.ds(home, home_rows), :]
                branch_away[...] = branch[pl.ds(away, away_rows), :].astype(BF16)

    part_specs = [pl.BlockSpec((part.shape[0], rows, BOTH), lambda i, *_: (0, 0, i + first)) for part in parts]
    grad_spec = pl.BlockSpec((slots, rows, BOTH), lambda i, *_: (0, 0, i))
    square = (tokens, width)
    table = whole((tokens, PAIR))
    in_specs = [
        once(square), once(square), ANY, ANY, table, table, table,
        pl.BlockSpec((1, TRIPLE), lambda i, *_: (0, i + first)),
    ] + part_specs
    operands = [n1, dy, n1t, dyt, *tables, bias, *parts]
    out_specs = [grad_spec] * outs + [pl.BlockSpec((1, TRIPLE), lambda i, *_: (0, i))]
    out_shape = [shape_of((slots, rows, BOTH * pairs), BF16)] * outs + [shape_of((1, TRIPLE * pairs), F32)]
    scratch = [
        pltpu.VMEM((width, BOTH), BF16), pltpu.VMEM((tokens, TRIPLE), BF16), pltpu.VMEM((tokens, PAIR), BF16),
        pltpu.VMEM((PAIR, tokens), F32), pltpu.VMEM((PAIR, tokens), F32),
        pltpu.VMEM((tokens, HD), F32), pltpu.VMEM((tokens, HD), F32),
        pltpu.VMEM((width, BOTH), BF16), pltpu.VMEM((width, tokens), BF16), pltpu.VMEM((width, tokens), BF16),
        pltpu.SemaphoreType.DMA((6,)),
    ]
    in_specs += [ANY] * len(init)
    operands += list(init)
    home, away = (home_rows, width), (away_rows, width)
    if last:
        share, hat, gain = final
        in_specs += [ANY, ANY, whole((1, width))]
        operands += [share, hat, gain[None]]
        out_specs += [whole((2, width)), whole(home), whole(home)]
        out_shape += [shape_of((2, width), F32), shape_of(home, F32), shape_of(home, F32)]
        if shared:
            early, late = (early_rows, width), (away_rows - early_rows, width)
            out_specs += [whole(early), whole(late), pl.BlockSpec((away_rows, PAIR), lambda i, *_: (0, i))]
            out_shape += [shape_of(early, BF16), shape_of(late, BF16), shape_of((away_rows, PAIR * pairs), BF16)]
        scratch += [
            pltpu.VMEM(square, F32), pltpu.VMEM(square, F32), pltpu.VMEM(square, BF16), pltpu.VMEM((tokens, PAIR), BF16)
        ]
    else:
        out_specs += [whole(square), whole(home), whole(away)]
        out_shape += [shape_of(square, F32), shape_of(home, F32), shape_of(away, BF16)]
        scratch += [pltpu.VMEM(square, F32)]
    in_specs += [ANY] * len(after)
    operands += list(after)
    return pl.pallas_call(
        kernel,
        grid_spec=pltpu.PrefetchScalarGridSpec(
            num_scalar_prefetch=1, grid=(pairs,), in_specs=in_specs, out_specs=out_specs, scratch_shapes=scratch
        ),
        out_shape=out_shape,
        compiler_params=pltpu.CompilerParams(vmem_limit_bytes=VMEM_BYTES),
        cost_estimate=pl.CostEstimate(
            flops=pairs * 20 * tokens * width * BOTH, transcendentals=pairs * tokens * tokens,
            bytes_accessed=32 * tokens * width,
        ),
        name="attention_both_ways",
    )(order, *operands)


def swap_dp(array, bits):
    count = lax.axis_size("dp")
    return lax.ppermute(array, "dp", [(i, i ^ bits) for i in range(count)])


def swap_tensor(array):
    return lax.ppermute(array, "tensor", [(0, 1), (1, 0)])


def hold(arrays, *after):
    def kernel(*refs):
        del refs

    return pl.pallas_call(
        kernel,
        in_specs=[ANY] * (len(arrays) + len(after)),
        out_specs=[ANY] * len(arrays),
        out_shape=[shape_of(a.shape, a.dtype) for a in arrays],
        input_output_aliases={i: i for i in range(len(arrays))},
        name="hold",
    )(*arrays, *after)


def join(pieces, *after):
    rows, width = pieces[0].shape
    block = min(width, 1024)
    count = len(pieces)

    def kernel(*refs):
        out = refs[-1]
        for index in range(count):
            out[index] = refs[index][...]

    return pl.pallas_call(
        kernel,
        grid=(width // block,),
        in_specs=[pl.BlockSpec((rows, block), lambda i: (0, i))] * count + [ANY] * len(after),
        out_specs=pl.BlockSpec((count, rows, block), lambda i: (0, 0, i)),
        out_shape=shape_of((count, rows, width), BF16),
        name="join",
    )(*pieces, *after)


def interleave(pairs, chunks):
    rows = pairs[0][0].shape[0]
    layouts = []
    for (one, other, size_one, size_other), count in zip(pairs, chunks):
        steps = one.shape[1] // size_one // count
        layouts.append((size_one, size_other, steps, count))

    def kernel(*refs):
        ins, outs = refs[: 2 * len(pairs)], list(refs[2 * len(pairs) :])
        for index, (size_one, size_other, steps, count) in enumerate(layouts):
            one, other = ins[2 * index : 2 * index + 2]
            size = size_one + size_other
            for chunk in range(count):
                out = outs.pop(0)
                for step in range(steps):
                    at = chunk * steps + step
                    out[:, step * size : step * size + size_one] = one[:, at * size_one : (at + 1) * size_one]
                    out[:, step * size + size_one : (step + 1) * size] = other[:, at * size_other : (at + 1) * size_other]

    return pl.pallas_call(
        kernel,
        out_shape=[
            shape_of((rows, steps * (size_one + size_other)), BF16)
            for size_one, size_other, steps, count in layouts
            for _ in range(count)
        ],
        name="interleave",
    )(*[array for pair in pairs for array in pair[:2]])


def finish_weights(sources, size_one, size_other):
    size = size_one + size_other
    counts = [len(source) for source in sources]
    widths = [source[0].shape[-1] for source in sources]
    arrays = [array.reshape(array.shape[-2:]) for source in sources for array in source]
    rows = arrays[0].shape[0]
    steps = sum(widths) // size

    def kernel(*refs):
        ins, one, other = list(refs[:-2]), refs[-2], refs[-1]
        at = 0
        for count, width in zip(counts, widths):
            total = ins.pop(0)[...].astype(F32)
            for _ in range(count - 1):
                total = total + ins.pop(0)[...].astype(F32)
            for step in range(width // size):
                base = step * size
                one[:, at * size_one : (at + 1) * size_one] = total[:, base : base + size_one]
                other[:, at * size_other : (at + 1) * size_other] = total[:, base + size_one : base + size]
                at += 1

    return pl.pallas_call(
        kernel,
        out_shape=[shape_of((rows, steps * size_one), F32), shape_of((rows, steps * size_other), F32)],
        name="finish_weights",
    )(*arrays)


def finish_output(inputs, branches, biases, context=None, weights=None, column=0):
    rows, width = inputs.shape
    block = min(rows, 256)
    n_branches = len(branches)
    inner = 0 if context is None else context.shape[1]

    def kernel(x, bias, *refs):
        total = x[...].astype(F32) + bias[0:1, :] + bias[1:2, :]
        for ref in refs[:n_branches]:
            total = total + ref[...].astype(F32)
        if inner:
            total = total + nt(refs[n_branches][...], refs[n_branches + 1][...])
        refs[-1][...] = total.astype(BF16)

    spec = pl.BlockSpec((block, width), lambda i: (i, 0))
    in_specs = [spec, pl.BlockSpec((2, width), lambda i: (0, 0))] + [spec] * n_branches
    operands = [inputs, biases, *branches]
    if inner:
        in_specs += [
            pl.BlockSpec((block, inner), lambda i: (i, 0)), pl.BlockSpec((width, inner), lambda i: (0, column // inner))
        ]
        operands += [context, weights]
    return pl.pallas_call(
        kernel,
        grid=(rows // block,),
        in_specs=in_specs,
        out_specs=spec,
        out_shape=shape_of((rows, width), BF16),
        name="finish_output",
    )(*operands)


def finish_input(inputs, cotangent, home, others, *after):
    rows, width = inputs.shape
    block = min([rows, 128] + [other.shape[0] for other in others])
    starts = np.cumsum([0] + [other.shape[0] // block for other in others])
    count = len(others)

    def kernel(x, dy, home, *refs):
        step = pl.program_id(0)
        share = home[...].astype(F32)
        for index in range(count):
            mine = (step >= starts[index]) & (step < starts[index + 1])
            share = share + jnp.where(mine, refs[index][...].astype(F32), 0.0)
        xhat, rate = normalize(x[...].astype(F32))
        lead = jnp.mean(share, axis=-1, keepdims=True)
        along = jnp.mean(share * xhat, axis=-1, keepdims=True)
        refs[-1][...] = dy[...].astype(F32) + rate * (share - lead - xhat * along)

    def part(index):
        low, high = int(starts[index]), int(starts[index + 1])
        return pl.BlockSpec((block, width), lambda i: (jnp.clip(i - low, 0, high - low - 1), 0))

    spec = pl.BlockSpec((block, width), lambda i: (i, 0))
    return pl.pallas_call(
        kernel,
        grid=(rows // block,),
        in_specs=[spec] * 3 + [part(index) for index in range(count)] + [ANY] * len(after),
        out_specs=spec,
        out_shape=shape_of((rows, width), F32),
        name="finish_input",
    )(inputs, cotangent, home, *others, *after)


def flatten_rows(arrays):
    total = sum(a.shape[0] * a.shape[1] for a in arrays)

    def kernel(*refs):
        out, at = refs[-1], 0
        for ref in refs[:-1]:
            count, width = ref.shape
            for row in range(count):
                out[:, at : at + width] = ref[row : row + 1, :]
                at += width

    return pl.pallas_call(kernel, out_shape=shape_of((1, total), F32), name="flatten_rows")(*arrays)


def add_split(left, right, sizes):
    count, rows, width = left.shape
    block = min(width, 512)

    def kernel(left, right, *outs):
        at = 0
        for size, out in zip(sizes, outs):
            total = left[at : at + size].astype(F32) + right[at : at + size].astype(F32)
            out[...] = total.astype(BF16)
            at += size

    spec = pl.BlockSpec((count, rows, block), lambda i: (0, 0, i))
    return pl.pallas_call(
        kernel,
        grid=(width // block,),
        in_specs=[spec, spec],
        out_specs=[pl.BlockSpec((size, rows, block), lambda i: (0, 0, i)) for size in sizes],
        out_shape=[shape_of((size, rows, width), BF16) for size in sizes],
        name="add_split",
    )(left, right)


def relative_order(weights):
    slots = np.arange(16)
    bits = (slots % 4) * 4 + (slots // 4 % 2) * weights[0] + (slots // 8) * weights[1]
    return jnp.asarray(bits, jnp.int32) ^ lax.axis_index("dp").astype(jnp.int32)


def gather_lines(piece, *after):
    return join([piece] + [swap_dp(piece, 4 * s) for s in (1, 2, 3)], *after)


def send_lines(lines):
    return [lines[0]] + [swap_dp(lines[s], 4 * s) for s in (1, 2, 3)]


def on_device(
    inputs, attn_gain, attn_bias, mlp_gain, mlp_bias, w_qkv, b_qkv, w_out, b_out, w_up, b_up, w_down, b_down, cotangent
):
    own_rows, width = inputs.shape
    units = w_up.shape[1]
    columns = w_qkv.shape[1]
    pairs = columns // TRIPLE
    piece_rows = w_up.shape[0]
    n_dp, n_tensor = lax.axis_size("dp"), lax.axis_size("tensor")
    by_hand = n_dp == 16 and n_tensor == 2
    block = min(UNIT_BLOCK, units)
    gains = jnp.stack([attn_gain, attn_bias, mlp_gain, mlp_bias])
    natural = jnp.arange(n_dp, dtype=jnp.int32)
    side = lax.axis_index("tensor").astype(jnp.int32)
    tables = rotary_tables(own_rows * n_tensor)

    def full_gather(piece):
        return lax.all_gather(piece, "dp", axis=0, tiled=True).reshape(n_dp, piece_rows, piece.shape[1])

    def full_scatter(parts):
        return lax.psum_scatter(parts.reshape(width, parts.shape[2]), "dp", scatter_dimension=0, tiled=True)

    biases = jnp.stack([b_out, b_down])
    if by_hand:
        sides = jnp.zeros((n_dp,), jnp.int32).at[0].set(side).at[1].set(1 - side)
        arrive, leave = relative_order((1, 2)), relative_order((2, 1))
        place = side[None]
        piece_a, piece_b, attn_piece = interleave(
            [(w_up, w_down.T, block, block), (w_qkv, w_out.T, TRIPLE, PAIR)], (2, 1)
        )
        first = pairs // 2
        later = (pairs - first) * PAIR
        x_other = swap_tensor(inputs)
        out_other = swap_tensor(w_out.T[:, first * PAIR :])
        lines_a = gather_lines(piece_a, x_other, out_other)
        held_dy, piece_b = hold([cotangent, piece_b], lines_a)
        dy_other = swap_tensor(held_dy)
        lines_b = gather_lines(piece_b)
        n1, n2, n1t, n2t, hat = two_sided(norm_kernel, place, inputs, x_other, [gains], (2, 1), 2)
        attn_piece = jnp.concatenate([attn_piece, out_other], axis=1)
        across_a, lines_b, attn_piece = hold([swap_dp(lines_a, 2), lines_b, attn_piece], n1, dy_other)
        attn_wide = full_gather(attn_piece)
        attn_parts = [attn_wide]
        parts_a = [lines_a, swap_dp(lines_a, 1), across_a, swap_dp(across_a, 1)]
        dy, dyt, dy_sum = two_sided(turn_kernel, place, cotangent, dy_other, [], (1, 0), 1, 1)

        order = jnp.stack([arrive, natural])
        buffer, gb_a, branch, dn2 = mlp_call(
            order, n2, n2t, dy, dyt, b_up[None, : units // 2], parts_a, chunk=(0, 2), after=[lines_b]
        )
        (across_b,) = hold([swap_dp(lines_b, 2)], gb_a)
        parts_b = [lines_b, swap_dp(lines_b, 1), across_b, swap_dp(across_b, 1)]
        wide, gb_b, branch, share, sums_two = mlp_call(
            order, n2, n2t, dy, dyt, b_up[None, units // 2 :], parts_b, chunk=(1, 2), buffer=buffer,
            init=(branch, dn2), final=(hat, mlp_gain),
        )
        mlp_sum = full_scatter(wide)
        attn_order = jnp.stack([natural, leave, sides])
        keep_c, send_c, gb_c, dn1, branch_home, branch_away = attention_call(
            attn_order, n1, n1t, dy, dyt, tables, b_qkv[None], attn_parts, 2, 0, first, (branch,), own_rows
        )
        branch_other = swap_tensor(branch_away)
        low_c, high_c = add_split(keep_c, swap_dp(send_c, 1), (4, 4))
        keep_d, send_d, gb_d, sums_one, branch_home, share_home, share_first, share_second, ctx_away = attention_call(
            attn_order, n1, n1t, dy, dyt, tables, b_qkv[None], attn_parts, 2, first, pairs - first,
            (branch_home, dn1), own_rows, final=(share, hat, attn_gain), after=[high_c],
        )
        across_c, branch_other, ctx_away, share_first, share_second, send_d, gb_d = hold(
            [
                swap_dp(high_c, 2), branch_other, ctx_away, share_first, share_second, send_d, gb_d,
            ]
        )
        ctx_other = swap_tensor(ctx_away)
        share_first = swap_tensor(share_first)
        low_d, high_d = add_split(keep_d, swap_dp(send_d, 1), (4, 4))
        sent_c = send_lines(add_split(low_c, across_c, (1, 1, 1, 1)))
        small = flatten_rows([gb_c, gb_d, gb_a, gb_b, sums_one, sums_two, dy_sum])
        small = small + swap_dp(small, 1)
        (small,) = hold([small], high_d)
        small = small + swap_dp(small, 2)
        small = small + swap_tensor(jnp.where(jnp.arange(small.shape[1]) < columns + units, 0.0, small))
        output = finish_output(
            inputs, [branch_home, branch_other], biases, ctx_other, attn_wide.reshape(width, -1), columns + pairs * PAIR
        )
        across_d, share_first, small, share_second, *sent_c = hold(
            [swap_dp(high_d, 2), share_first, small, share_second, *sent_c]
        )
        lines_d = add_split(low_d, across_d, (1, 1, 1, 1))
        sent_d = send_lines(lines_d)
        share_second, small = hold([share_second, small], *lines_d)
        share_second = swap_tensor(share_second)
        small = small + swap_dp(small, 4) + swap_dp(small, 8) + swap_dp(small, 12)
        grad_up, grad_down_t = finish_weights([[mlp_sum]], block, block)
        attn_sources = [sent_c, sent_d]
        grad_inputs = finish_input(inputs, cotangent, share_home, [share_first, share_second], grad_up, output)
        small = small[0]
        tail = small[columns + units :]
    else:
        mlp_piece, attn_piece = interleave(
            [(w_up, w_down.T, block, block), (w_qkv, w_out.T, TRIPLE, PAIR)], (1, 1)
        )
        order = jnp.stack([natural, natural, jnp.zeros_like(natural)])
        x = lax.all_gather(inputs, "tensor", axis=0, tiled=True)
        dy = lax.all_gather(cotangent, "tensor", axis=0, tiled=True)
        mlp_parts = [full_gather(mlp_piece)]
        attn_parts = [full_gather(attn_piece)]
        rows = x.shape[0]
        place = jnp.zeros((1,), jnp.int32)
        n1, n2, n1t, n2t, hat = two_sided(
            norm_kernel, place, x[: rows // 2], x[rows // 2 :], [gains], (2, 1), 2
        )
        dy, dyt, _ = two_sided(turn_kernel, place, dy[: rows // 2], dy[rows // 2 :], [], (1, 0), 1, 1)
        wide, gb_up, branch, share, sums_two = mlp_call(
            order[:2], n2, n2t, dy, dyt, b_up[None], mlp_parts, final=(hat, mlp_gain)
        )
        narrow, gb_qkv, sums_one, branch, share = attention_call(
            order, n1, n1t, dy, dyt, tables, b_qkv[None], attn_parts, 1, 0, pairs, (branch,), rows,
            final=(share, hat, attn_gain),
        )
        grad_up, grad_down_t = finish_weights([[full_scatter(wide)]], block, block)
        attn_sources = [[full_scatter(narrow)]]
        share = lax.psum_scatter(share.astype(BF16), "tensor", scatter_dimension=0, tiled=True)
        branch = lax.psum_scatter(branch.astype(BF16), "tensor", scatter_dimension=0, tiled=True)
        output = finish_output(inputs, [branch], biases)
        grad_inputs = finish_input(inputs, cotangent, share, [])
        small = lax.psum(jnp.concatenate([gb_qkv[0], gb_up[0]]), "dp")
        own_sum = jnp.sum(cotangent.astype(F32), axis=0)
        tail = lax.psum(jnp.concatenate([sums_one.reshape(-1), sums_two.reshape(-1), own_sum]), ("dp", "tensor"))

    sums = tail.reshape(5, width)
    grad_qkv, grad_out_t = finish_weights(attn_sources, TRIPLE, PAIR)
    return (
        output,
        grad_inputs,
        sums[0],
        sums[1],
        sums[2],
        sums[3],
        grad_qkv,
        small[:columns],
        grad_out_t.T,
        sums[4],
        grad_up,
        small[columns : columns + units],
        grad_down_t.T,
        sums[4],
    )


def solution(mesh):
    rows = P(("dp", "tensor"), None)
    return jax.shard_map(
        on_device,
        mesh=mesh,
        in_specs=(
            rows, P(), P(), P(), P(), P("dp", "tensor"), P("tensor"), P("tensor", "dp"), P(),
            P("dp", "tensor"), P("tensor"), P("tensor", "dp"), P(), rows,
        ),
        out_specs=(
            rows, rows, P(), P(), P(), P(), P("dp", "tensor"), P("tensor"), P("tensor", "dp"), P(),
            P("dp", "tensor"), P("tensor"), P("tensor", "dp"), P(),
        ),
        check_vma=False,
    )
```

```python
import jax
import jax.numpy as jnp
import numpy as np
from jax import lax
from jax.experimental import pallas as pl
from jax.experimental.pallas import tpu as pltpu
from jax.sharding import PartitionSpec as P

HD = 64
ROT = 16
SEQ = 1024
EPSILON = 1e-05
PAIR = 2 * HD
TRIPLE = 6 * HD
BOTH = TRIPLE + PAIR
Q_BLOCK = 256
ROW_BLOCK = 256
UNIT_BLOCK = 512
VMEM_BYTES = 60 * 1024 * 1024
F32 = jnp.float32
BF16 = jnp.bfloat16
ANY = pl.BlockSpec(memory_space=pl.ANY)


def normalize(rows):
    average = jnp.mean(rows, axis=-1, keepdims=True)
    centered = rows - average
    spread = jnp.mean(centered * centered, axis=-1, keepdims=True)
    rate = lax.rsqrt(spread + EPSILON)
    return centered * rate, rate


def rotary_tables(count):
    positions = (np.arange(count) % SEQ).astype(np.float32)
    inverse = (10000.0 ** (-(2.0 * np.arange(ROT // 2)) / ROT)).astype(np.float32)
    angles = (positions[:, None] * inverse[None, :]).astype(np.float64)
    cosine, sine = np.cos(angles), np.sin(angles)
    none = np.zeros_like(sine)
    rest = np.zeros((count, HD - ROT))
    keep = np.concatenate([cosine, cosine, rest + 1.0], axis=1)
    down = np.concatenate([none, sine, rest], axis=1)
    up = np.concatenate([-sine, none, rest], axis=1)
    return tuple(jnp.asarray(np.concatenate([t, t], axis=1), F32) for t in (keep, down, up))


def nn(left, right):
    return jnp.dot(left, right, preferred_element_type=F32)


def nt(left, right):
    return lax.dot_general(left, right, (((1,), (1,)), ((), ())), preferred_element_type=F32)


class Copies:
    def __init__(self, sem):
        self.sem = sem
        self.count = 0
        self.open = []

    def start(self, source, target):
        copy = pltpu.make_async_copy(source, target, self.sem.at[self.count])
        self.count += 1
        copy.start()
        self.open.append(copy)
        return copy

    def rows_in(self, order, parts, columns, target, into):
        copies, at = [], 0
        for part in parts:
            count, rows, _ = part.shape
            for slot in range(count):
                place = pl.ds(pl.multiple_of(order[0, at + slot] * rows, rows), rows)
                copies.append(self.start(part.at[slot, :, columns], target.at[place, into]))
            at += count
        return copies

    def rows_out(self, order, source, outof, parts, columns):
        at = 0
        for part in parts:
            count, rows, _ = part.shape
            for slot in range(count):
                place = pl.ds(pl.multiple_of(order[1, at + slot] * rows, rows), rows)
                self.start(source.at[place, outof], part.at[slot, :, columns])
            at += count

    def wait(self, *copies):
        for copy in copies:
            if copy in self.open:
                self.open.remove(copy)
                copy.wait()

    def wait_all(self):
        self.wait(*list(self.open))


def whole(shape):
    return pl.BlockSpec(shape, lambda i, *_: (0,) * len(shape))


def once(shape):
    return pl.BlockSpec(shape, lambda i, *_: (0,) * len(shape), pipeline_mode=pl.Buffered(1))


def shape_of(shape, dtype):
    return jax.ShapeDtypeStruct(shape, dtype)


def norm_kernel(place, own, other, gains, normed_one, normed_two, one_t, two_t, hat):
    mine = pl.program_id(0) // (pl.num_programs(0) // 2) == place[0]
    rows = jnp.where(mine, own[...], other[...]).astype(F32)
    xhat, _ = normalize(rows)
    one = (xhat * gains[0:1, :] + gains[1:2, :]).astype(BF16)
    two = (xhat * gains[2:3, :] + gains[3:4, :]).astype(BF16)
    normed_one[...] = one
    normed_two[...] = two
    one_t[...] = one.T
    two_t[...] = two.T
    hat[...] = xhat.astype(BF16)


def turn_kernel(place, own, other, rows_out, turned, total):
    mine = pl.program_id(0) // (pl.num_programs(0) // 2) == place[0]
    rows = jnp.where(mine, own[...], other[...])
    rows_out[...] = rows
    turned[...] = rows.T

    @pl.when(pl.program_id(0) == 0)
    def _():
        total[...] = jnp.zeros_like(total)

    @pl.when(mine)
    def _():
        total[...] += jnp.sum(own[...].astype(F32), axis=0, keepdims=True)


def two_sided(kernel, place, own, other, extra, straight, flipped, summed=0):
    rows, width = own.shape
    steps = 2 * rows // ROW_BLOCK
    half = pl.BlockSpec((ROW_BLOCK, width), lambda i, *_: (i % (steps // 2), 0))
    row_spec = pl.BlockSpec((ROW_BLOCK, width), lambda i, *_: (i, 0))
    col_spec = pl.BlockSpec((width, ROW_BLOCK), lambda i, *_: (0, i))
    before, after = straight
    return pl.pallas_call(
        kernel,
        grid_spec=pltpu.PrefetchScalarGridSpec(
            num_scalar_prefetch=1,
            grid=(steps,),
            in_specs=[half, half] + [whole(e.shape) for e in extra],
            out_specs=[row_spec] * before + [col_spec] * flipped + [row_spec] * after + [whole((1, width))] * summed,
        ),
        out_shape=[shape_of((2 * rows, width), BF16)] * before
        + [shape_of((width, 2 * rows), BF16)] * flipped
        + [shape_of((2 * rows, width), BF16)] * after
        + [shape_of((1, width), F32)] * summed,
        compiler_params=pltpu.CompilerParams(vmem_limit_bytes=VMEM_BYTES),
        name=kernel.__name__,
    )(place, own, other, *extra)


def mlp_call(order, n2, n2t, dy, dyt, bias, parts, chunk=(0, 1), buffer=None, init=None, final=None, after=()):
    tokens, width = n2.shape
    _, rows, both = parts[0].shape
    units = both // 2
    block = min(UNIT_BLOCK, units)
    steps = units // block
    n_parts = len(parts)
    slots = sum(part.shape[0] for part in parts)
    chunks = [slice(start, start + ROW_BLOCK) for start in range(0, tokens, ROW_BLOCK)]

    def kernel(order, *refs):
        refs = list(refs)
        take = lambda n: [refs.pop(0) for _ in range(n)]
        take(0 if buffer is None else 1)
        n2_hbm, dy_hbm, n2t_hbm, dyt_hbm, bias = take(5)
        weights = take(n_parts)
        starts = take(2 if init is not None else 0)
        hat_hbm, gain = take(2) if final is not None else (None, None)
        take(len(after))
        grads, gbias, branch_hbm, dnormed_hbm = take(4)
        sums = take(1)[0] if final is not None else None
        n2, dy, n2t, dyt, w, act, dhid, gwide, branch, dnormed, sem = take(11)
        hat = take(1)[0] if final is not None else None
        copies = Copies(sem)
        up = [slice(2 * i * block, (2 * i + 1) * block) for i in range(steps)]
        down = [slice((2 * i + 1) * block, (2 * i + 2) * block) for i in range(steps)]
        unit = [slice(i * block, (i + 1) * block) for i in range(steps)]
        need_up, need_down = [], []
        for i in range(steps):
            need_up.append(copies.rows_in(order, weights, up[i], w, up[i]))
            if i == 0:
                need_up[0].append(copies.start(n2_hbm, n2))
            need_down.append(copies.rows_in(order, weights, down[i], w, down[i]))
            if i == 0:
                need_down[0].append(copies.start(dy_hbm, dy))
        begun = []
        if init is not None:
            begun += [copies.start(starts[0], branch), copies.start(starts[1], dnormed)]
        if final is not None:
            begun += [copies.start(hat_hbm, hat)]
        need_n2t, need_dyt = copies.start(n2t_hbm, n2t), copies.start(dyt_hbm, dyt)
        for i in range(steps):
            total = jnp.zeros((1, block), F32)
            copies.wait(*need_up[i])
            for index, at in enumerate(chunks):
                hidden = nn(n2[at, :], w[:, up[i]]) + bias[:, unit[i]]
                if index == 0:
                    copies.wait(*need_down[i])
                dactive = nn(dy[at, :], w[:, down[i]])
                below = 0.5 + 0.5 * lax.erf(hidden * 0.7071067811865476)
                density = jnp.exp(hidden * hidden * -0.5) * 0.3989422804014327
                dhidden = (dactive * (below + hidden * density)).astype(BF16)
                act[at, unit[i]] = (hidden * below).astype(BF16)
                dhid[at, unit[i]] = dhidden
                total += jnp.sum(dhidden.astype(F32), axis=0, keepdims=True)
            gbias[:, unit[i]] = total
        copies.wait(*begun)
        hat_sum = direct_sum = jnp.zeros((1, width), F32)
        for at in chunks:
            direct = sum(nt(dhid[at, unit[i]], w[:, up[i]]) for i in range(steps))
            mixed = sum(nt(act[at, unit[i]], w[:, down[i]]) for i in range(steps))
            if init is not None:
                direct = direct + dnormed[at, :]
                mixed = mixed + branch[at, :]
            if final is not None:
                hat_sum += jnp.sum(direct * hat[at, :].astype(F32), axis=0, keepdims=True)
                direct_sum += jnp.sum(direct, axis=0, keepdims=True)
                direct = direct * gain[...]
            dnormed[at, :] = direct
            branch[at, :] = mixed
            copies.start(dnormed.at[at, :], dnormed_hbm.at[at, :])
            copies.start(branch.at[at, :], branch_hbm.at[at, :])
        if final is not None:
            sums[0:1, :] = hat_sum
            sums[1:2, :] = direct_sum
        copies.wait(need_n2t, need_dyt)
        for i in range(steps):
            both_at = slice(2 * i * block, (2 * i + 2) * block)
            shifted = slice(chunk[0] * both + 2 * i * block, chunk[0] * both + (2 * i + 2) * block)
            gwide[:, up[i]] = nn(n2t[...], dhid[:, unit[i]]).astype(BF16)
            gwide[:, down[i]] = nn(dyt[...], act[:, unit[i]]).astype(BF16)
            copies.rows_out(order, gwide, both_at, [grads], shifted)
        copies.wait_all()

    square = (tokens, width)
    in_specs = [ANY] * 4 + [whole((1, units))] + [ANY] * n_parts
    operands = [n2, dy, n2t, dyt, bias, *parts]
    out_specs = [ANY, whole((1, units)), ANY, ANY]
    out_shape = [
        shape_of((slots, rows, both * chunk[1]), BF16),
        shape_of((1, units), F32), shape_of(square, F32), shape_of(square, F32),
    ]
    if buffer is not None:
        in_specs = [ANY] + in_specs
        operands = [buffer] + operands
    scratch = [
        pltpu.VMEM(square, BF16), pltpu.VMEM(square, BF16),
        pltpu.VMEM((width, tokens), BF16), pltpu.VMEM((width, tokens), BF16),
        pltpu.VMEM((width, both), BF16), pltpu.VMEM((tokens, units), BF16), pltpu.VMEM((tokens, units), BF16),
        pltpu.VMEM((width, both), BF16), pltpu.VMEM(square, F32), pltpu.VMEM(square, F32),
        pltpu.SemaphoreType.DMA((3 * slots * steps + 2 * len(chunks) + 8,)),
    ]
    if init is not None:
        in_specs += [ANY, ANY]
        operands += list(init)
    if final is not None:
        hat, gain = final
        in_specs += [ANY, whole((1, width))]
        operands += [hat, gain[None]]
        out_specs += [whole((2, width))]
        out_shape += [shape_of((2, width), F32)]
        scratch += [pltpu.VMEM(square, BF16)]
    in_specs += [ANY] * len(after)
    operands += list(after)
    return pl.pallas_call(
        kernel,
        grid_spec=pltpu.PrefetchScalarGridSpec(
            num_scalar_prefetch=1, grid=(1,), in_specs=in_specs, out_specs=out_specs, scratch_shapes=scratch
        ),
        out_shape=out_shape,
        input_output_aliases={} if buffer is None else {1: 0},
        compiler_params=pltpu.CompilerParams(vmem_limit_bytes=VMEM_BYTES),
        cost_estimate=pl.CostEstimate(
            flops=12 * tokens * width * units, transcendentals=2 * tokens * units, bytes_accessed=32 * tokens * width
        ),
        name="mlp_both_ways",
    )(order, *operands)


def attention_call(order, n1, n1t, dy, dyt, tables, bias, parts, outs, call, pairs, init, home_rows, final=None, after=()):
    tokens, width = n1.shape
    rows = parts[0].shape[1]
    n_parts = len(parts)
    slots = sum(part.shape[0] for part in parts) // outs
    half = ROT // 2
    away_rows = tokens - home_rows
    last = final is not None
    shared = away_rows > 0
    share_cuts = [0, away_rows // 4, away_rows]
    wide, narrow = pairs * TRIPLE, pairs * PAIR
    size = wide + narrow
    chunks = [slice(start, start + ROW_BLOCK) for start in range(0, tokens, ROW_BLOCK)]

    def kernel(order, *refs):
        refs = list(refs)
        take = lambda n: [refs.pop(0) for _ in range(n)]
        n1_hbm, dy_hbm, n1t_hbm, dyt_hbm, keep, down, up, bias = take(8)
        weights = take(n_parts)
        starts = take(len(init))
        share_hbm, hat_hbm, gain = take(3) if last else (None, None, None)
        take(len(after))
        grads = take(outs)
        (gbias,) = take(1)
        if last:
            sums, branch_hbm, share_home = take(3)
            outs_away = take(3) if shared else []
        else:
            dnormed_hbm, branch_hbm, outs_away = take(2) + [take(1)]
        n1, dy, n1t, dyt, w, turned, dctx, ctx_t, dq_t, dkv, dmixed, context, gwide, dnormed, branch, sem = take(16)
        away_low = take(1)[0] if shared else None
        share, hat = take(2) if last else (None, None)
        home = pl.multiple_of(order[2, 0] * home_rows, home_rows)
        away = pl.multiple_of(order[2, 1] * away_rows, 16)
        copies = Copies(sem)
        everything = slice(0, size)
        need_w = copies.rows_in(order, weights, slice(call * size, (call + 1) * size), w, everything)
        need_n1 = copies.start(n1_hbm, n1)
        need_dy = copies.start(dy_hbm, dy)
        begun = [copies.start(start, total) for start, total in zip(starts, (branch, dnormed))]
        if last:
            begun += [copies.start(share_hbm, share), copies.start(hat_hbm, hat)]
        need_t = [copies.start(n1t_hbm, n1t), copies.start(dyt_hbm, dyt)]

        def rotate(rows, at, sign):
            lane = lax.broadcasted_iota(jnp.int32, rows[0].shape, 1)
            groups = []
            for index, r in enumerate(rows):
                shift = pltpu.roll(r, half, 1) * down[at, :] + pltpu.roll(r, PAIR - half, 1) * up[at, :]
                turn = r * keep[at, :] + sign * shift
                place = index % 3
                groups.append(turn if place == 0 else jnp.where((lane >= HD) == (place == 1), turn, r))
            return groups

        copies.wait(*need_w, need_n1)
        for at in chunks:
            mixed = nn(n1[at, :], w[:, :wide]) + bias[...]
            for index, group in enumerate(rotate([mixed[:, i * PAIR : (i + 1) * PAIR] for i in range(3 * pairs)], at, 1.0)):
                turned[at, index * PAIR : (index + 1) * PAIR] = group.astype(BF16)
        copies.wait(need_dy)
        dctx[...] = nn(dy[...], w[:, wide:]).astype(BF16)
        behind = lax.broadcasted_iota(jnp.int32, (Q_BLOCK, Q_BLOCK), 0) > lax.broadcasted_iota(
            jnp.int32, (Q_BLOCK, Q_BLOCK), 1
        )
        blank = jnp.zeros((tokens, HD), BF16)
        dkv[...] = jnp.zeros_like(dkv)
        for pair in range(pairs):
            heads = []
            for head in range(2):
                base = pair * TRIPLE + head * 3 * HD
                query = turned[:, base : base + HD] * jnp.asarray(0.125, BF16)
                key = turned[:, base + HD : base + 2 * HD]
                value = turned[:, base + 2 * HD : base + 3 * HD]
                grad = dctx[:, pair * PAIR + head * HD : pair * PAIR + (head + 1) * HD]
                left = jnp.concatenate([query, blank], axis=1)
                right = jnp.concatenate([blank, grad], axis=1)
                heads.append((query, key, value, grad, key.T, value.T, left, right))
            for start in range(0, tokens, Q_BLOCK):
                stop = start + Q_BLOCK
                products = [
                    (nt(key[:stop], query[start:stop]), nt(value[:stop], grad[start:stop]))
                    for query, key, value, grad, *_ in heads
                ]
                mixes = []
                for scores, dprobs in products:
                    edge = jnp.where(behind, -1e30, scores[start:])
                    scores = edge if start == 0 else jnp.concatenate([scores[:start], edge], axis=0)
                    expos = jnp.exp(scores - jnp.max(scores, axis=0, keepdims=True))
                    probs = expos * (1.0 / jnp.sum(expos, axis=0, keepdims=True))
                    inner = jnp.sum(probs * dprobs, axis=0, keepdims=True)
                    mixes.append((probs.astype(BF16), (probs * (dprobs - inner)).astype(BF16)))
                for head, (low, dscores) in enumerate(mixes):
                    _, _, _, _, key_t, value_t, left, right = heads[head]
                    lines = slice(pair * PAIR + head * HD, pair * PAIR + (head + 1) * HD)
                    ctx_t[lines, start:stop] = nn(value_t[:, :stop], low)
                    dq_t[lines, start:stop] = nn(key_t[:, :stop], dscores) * 0.125
                    dkv[2 * pair + head, :stop, :] += nn(dscores, left[start:stop]) + nn(low, right[start:stop])
        context[...] = ctx_t[...].T.astype(BF16)
        if shared and last:
            copies.start(context.at[pl.ds(away, away_rows), :], outs_away[2])
        copies.wait(*begun)
        total = jnp.zeros((1, wide), F32)
        hat_sum = direct_sum = jnp.zeros((1, width), F32)
        for at in chunks:
            rows_before = []
            lane = lax.broadcasted_iota(jnp.int32, (ROW_BLOCK, PAIR), 1)
            for pair in range(pairs):
                dq = dq_t[pair * PAIR : (pair + 1) * PAIR, at].T
                swapped = pltpu.roll(dkv[2 * pair, at, :], HD, 1)
                rows_before += [
                    jnp.where(lane < HD, dq, swapped), jnp.where(lane < HD, swapped, dq), dkv[2 * pair + 1, at, :]
                ]
            low = jnp.concatenate(rotate(rows_before, at, -1.0), axis=1).astype(BF16)
            dmixed[at, :] = low
            total += jnp.sum(low.astype(F32), axis=0, keepdims=True)
            direct = nt(low, w[:, :wide])
            if len(init) > 1:
                direct = direct + dnormed[at, :]
            if last:
                hat_sum += jnp.sum(direct * hat[at, :].astype(F32), axis=0, keepdims=True)
                direct_sum += jnp.sum(direct, axis=0, keepdims=True)
                direct = direct * gain[...] + share[at, :]
            dnormed[at, :] = direct
            if not last:
                copies.start(dnormed.at[at, :], dnormed_hbm.at[at, :])
        gbias[...] = total
        if last:
            sums[0:1, :] = hat_sum
            sums[1:2, :] = direct_sum
            copies.start(dnormed.at[pl.ds(home, home_rows), :], share_home)
            if shared:
                away_low[...] = dnormed[pl.ds(away, away_rows), :].astype(BF16)
                for index in range(2):
                    copies.start(away_low.at[share_cuts[index] : share_cuts[index + 1], :], outs_away[index])
            branch[...] += nt(context[pl.ds(home, home_rows), :], w[:, wide:])
            copies.start(branch, branch_hbm)
        else:
            branch[...] += nt(context[...], w[:, wide:])
            copies.start(branch.at[pl.ds(home, home_rows), :], branch_hbm)
            away_low[...] = branch[pl.ds(away, away_rows), :].astype(BF16)
            copies.start(away_low, outs_away[0])
        copies.wait(*need_t)
        gwide[:, wide:] = nn(dyt[...], context[...]).astype(BF16)
        gwide[:, :wide] = nn(n1t[...], dmixed[...]).astype(BF16)
        copies.rows_out(order, gwide, everything, grads, everything)
        copies.wait_all()

    square = (tokens, width)
    table = whole((tokens, PAIR))
    home, away = (home_rows, width), (away_rows, width)
    in_specs = [ANY] * 4 + [table] * 3 + [pl.BlockSpec((1, wide), lambda i, *_: (0, call))] + [ANY] * (n_parts + len(init))
    operands = [n1, dy, n1t, dyt, *tables, bias, *parts, *init]
    out_specs = [ANY] * outs + [whole((1, wide))]
    out_shape = [shape_of((slots, rows, size), BF16)] * outs + [shape_of((1, wide), F32)]
    scratch = [
        pltpu.VMEM(square, BF16), pltpu.VMEM(square, BF16),
        pltpu.VMEM((width, tokens), BF16), pltpu.VMEM((width, tokens), BF16),
        pltpu.VMEM((width, size), BF16), pltpu.VMEM((tokens, wide), BF16), pltpu.VMEM((tokens, narrow), BF16),
        pltpu.VMEM((narrow, tokens), F32), pltpu.VMEM((narrow, tokens), F32),
        pltpu.VMEM((2 * pairs, tokens, PAIR), F32), pltpu.VMEM((tokens, wide), BF16), pltpu.VMEM((tokens, narrow), BF16),
        pltpu.VMEM((width, size), BF16), pltpu.VMEM(square, F32), pltpu.VMEM(home if last else square, F32),
        pltpu.SemaphoreType.DMA((2 * slots * outs + len(chunks) + 16,)),
    ]
    if shared:
        scratch += [pltpu.VMEM(away, BF16)]
    if last:
        share, hat, gain = final
        in_specs += [ANY, ANY, whole((1, width))]
        operands += [share, hat, gain[None]]
        out_specs += [whole((2, width)), ANY, ANY]
        out_shape += [shape_of((2, width), F32), shape_of(home, F32), shape_of(home, F32)]
        if shared:
            out_specs += [ANY] * 3
            out_shape += [shape_of((share_cuts[i + 1] - share_cuts[i], width), BF16) for i in range(2)]
            out_shape += [shape_of((away_rows, narrow), BF16)]
        scratch += [pltpu.VMEM(square, F32), pltpu.VMEM(square, BF16)]
    else:
        out_specs += [ANY] * 3
        out_shape += [shape_of(square, F32), shape_of(home, F32), shape_of(away, BF16)]
    in_specs += [ANY] * len(after)
    operands += list(after)
    return pl.pallas_call(
        kernel,
        grid_spec=pltpu.PrefetchScalarGridSpec(
            num_scalar_prefetch=1, grid=(1,), in_specs=in_specs, out_specs=out_specs, scratch_shapes=scratch
        ),
        out_shape=out_shape,
        compiler_params=pltpu.CompilerParams(vmem_limit_bytes=VMEM_BYTES),
        cost_estimate=pl.CostEstimate(
            flops=pairs * 20 * tokens * width * BOTH, transcendentals=pairs * tokens * tokens,
            bytes_accessed=32 * tokens * width,
        ),
        name="attention_both_ways",
    )(order, *operands)


def swap_dp(array, bits):
    count = lax.axis_size("dp")
    return lax.ppermute(array, "dp", [(i, i ^ bits) for i in range(count)])


def swap_tensor(array):
    return lax.ppermute(array, "tensor", [(0, 1), (1, 0)])


def hold(arrays, *after):
    def kernel(*refs):
        del refs

    return pl.pallas_call(
        kernel,
        in_specs=[ANY] * (len(arrays) + len(after)),
        out_specs=[ANY] * len(arrays),
        out_shape=[shape_of(a.shape, a.dtype) for a in arrays],
        input_output_aliases={i: i for i in range(len(arrays))},
        name="hold",
    )(*arrays, *after)


def join(pieces, *after):
    rows, width = pieces[0].shape
    block = min(width, 1024)
    count = len(pieces)

    def kernel(*refs):
        out = refs[-1]
        for index in range(count):
            out[index] = refs[index][...]

    return pl.pallas_call(
        kernel,
        grid=(width // block,),
        in_specs=[pl.BlockSpec((rows, block), lambda i: (0, i))] * count + [ANY] * len(after),
        out_specs=pl.BlockSpec((count, rows, block), lambda i: (0, 0, i)),
        out_shape=shape_of((count, rows, width), BF16),
        name="join",
    )(*pieces, *after)


def interleave(pairs, chunks):
    rows = pairs[0][0].shape[0]
    layouts = []
    for (one, other, size_one, size_other), count in zip(pairs, chunks):
        steps = one.shape[1] // size_one // count
        layouts.append((size_one, size_other, steps, count))

    def kernel(*refs):
        ins, outs = refs[: 2 * len(pairs)], list(refs[2 * len(pairs) :])
        for index, (size_one, size_other, steps, count) in enumerate(layouts):
            one, other = ins[2 * index : 2 * index + 2]
            size = size_one + size_other
            for chunk in range(count):
                out = outs.pop(0)
                for step in range(steps):
                    at = chunk * steps + step
                    out[:, step * size : step * size + size_one] = one[:, at * size_one : (at + 1) * size_one]
                    out[:, step * size + size_one : (step + 1) * size] = other[:, at * size_other : (at + 1) * size_other]

    return pl.pallas_call(
        kernel,
        out_shape=[
            shape_of((rows, steps * (size_one + size_other)), BF16)
            for size_one, size_other, steps, count in layouts
            for _ in range(count)
        ],
        name="interleave",
    )(*[array for pair in pairs for array in pair[:2]])


def finish_weights(sources, size_one, size_other):
    size = size_one + size_other
    counts = [len(source) for source in sources]
    widths = [source[0].shape[-1] for source in sources]
    arrays = [array.reshape(array.shape[-2:]) for source in sources for array in source]
    rows = arrays[0].shape[0]
    steps = sum(widths) // size

    def kernel(*refs):
        ins, one, other = list(refs[:-2]), refs[-2], refs[-1]
        at = 0
        for count, width in zip(counts, widths):
            total = ins.pop(0)[...].astype(F32)
            for _ in range(count - 1):
                total = total + ins.pop(0)[...].astype(F32)
            for step in range(width // size):
                base = step * size
                one[:, at * size_one : (at + 1) * size_one] = total[:, base : base + size_one]
                other[:, at * size_other : (at + 1) * size_other] = total[:, base + size_one : base + size]
                at += 1

    return pl.pallas_call(
        kernel,
        out_shape=[shape_of((rows, steps * size_one), F32), shape_of((rows, steps * size_other), F32)],
        name="finish_weights",
    )(*arrays)


def finish_output(inputs, branches, biases, context=None, weights=None, column=0):
    rows, width = inputs.shape
    block = min(rows, 256)
    n_branches = len(branches)
    inner = 0 if context is None else context.shape[1]

    def kernel(x, bias, *refs):
        total = x[...].astype(F32) + bias[0:1, :] + bias[1:2, :]
        for ref in refs[:n_branches]:
            total = total + ref[...].astype(F32)
        if inner:
            total = total + nt(refs[n_branches][...], refs[n_branches + 1][...])
        refs[-1][...] = total.astype(BF16)

    spec = pl.BlockSpec((block, width), lambda i: (i, 0))
    in_specs = [spec, pl.BlockSpec((2, width), lambda i: (0, 0))] + [spec] * n_branches
    operands = [inputs, biases, *branches]
    if inner:
        in_specs += [
            pl.BlockSpec((block, inner), lambda i: (i, 0)), pl.BlockSpec((width, inner), lambda i: (0, column // inner))
        ]
        operands += [context, weights]
    return pl.pallas_call(
        kernel,
        grid=(rows // block,),
        in_specs=in_specs,
        out_specs=spec,
        out_shape=shape_of((rows, width), BF16),
        name="finish_output",
    )(*operands)


def finish_input(inputs, cotangent, home, others, *after):
    rows, width = inputs.shape
    block = min([rows, 128] + [other.shape[0] for other in others])
    starts = np.cumsum([0] + [other.shape[0] // block for other in others])
    count = len(others)

    def kernel(x, dy, home, *refs):
        step = pl.program_id(0)
        share = home[...].astype(F32)
        for index in range(count):
            mine = (step >= starts[index]) & (step < starts[index + 1])
            share = share + jnp.where(mine, refs[index][...].astype(F32), 0.0)
        xhat, rate = normalize(x[...].astype(F32))
        lead = jnp.mean(share, axis=-1, keepdims=True)
        along = jnp.mean(share * xhat, axis=-1, keepdims=True)
        refs[-1][...] = dy[...].astype(F32) + rate * (share - lead - xhat * along)

    def part(index):
        low, high = int(starts[index]), int(starts[index + 1])
        return pl.BlockSpec((block, width), lambda i: (jnp.clip(i - low, 0, high - low - 1), 0))

    spec = pl.BlockSpec((block, width), lambda i: (i, 0))
    return pl.pallas_call(
        kernel,
        grid=(rows // block,),
        in_specs=[spec] * 3 + [part(index) for index in range(count)] + [ANY] * len(after),
        out_specs=spec,
        out_shape=shape_of((rows, width), F32),
        name="finish_input",
    )(inputs, cotangent, home, *others, *after)


def flatten_rows(arrays):
    total = sum(a.shape[0] * a.shape[1] for a in arrays)

    def kernel(*refs):
        out, at = refs[-1], 0
        for ref in refs[:-1]:
            count, width = ref.shape
            for row in range(count):
                out[:, at : at + width] = ref[row : row + 1, :]
                at += width

    return pl.pallas_call(kernel, out_shape=shape_of((1, total), F32), name="flatten_rows")(*arrays)


def add_split(pairs, sizes):
    count, rows, width = pairs[0][0].shape
    block = min(width, 512)
    steps = width // block

    def kernel(*refs):
        ins, outs = refs[: 2 * len(pairs)], refs[2 * len(pairs) :]
        for index in range(len(pairs)):
            left, right = ins[2 * index : 2 * index + 2]

            @pl.when(pl.program_id(0) // steps == index)
            def _():
                at = 0
                for size, out in zip(sizes, outs):
                    total = left[at : at + size].astype(F32) + right[at : at + size].astype(F32)
                    out[...] = total.astype(BF16)
                    at += size

    def part(index):
        return pl.BlockSpec((count, rows, block), lambda i: (0, 0, jnp.clip(i - index * steps, 0, steps - 1)))

    return pl.pallas_call(
        kernel,
        grid=(len(pairs) * steps,),
        in_specs=[part(index) for index in range(len(pairs)) for _ in range(2)],
        out_specs=[pl.BlockSpec((size, rows, block), lambda i: (0, 0, i)) for size in sizes],
        out_shape=[shape_of((size, rows, len(pairs) * width), BF16) for size in sizes],
        name="add_split",
    )(*[array for pair in pairs for array in pair])


def relative_order(weights):
    slots = np.arange(16)
    bits = (slots % 4) * 4 + (slots // 4 % 2) * weights[0] + (slots // 8) * weights[1]
    return jnp.asarray(bits, jnp.int32) ^ lax.axis_index("dp").astype(jnp.int32)


def gather_lines(piece, *after):
    return join([piece] + [swap_dp(piece, 4 * s) for s in (1, 2, 3)], *after)


def send_lines(lines):
    return [lines[0]] + [swap_dp(lines[s], 4 * s) for s in (1, 2, 3)]


def on_device(
    inputs, attn_gain, attn_bias, mlp_gain, mlp_bias, w_qkv, b_qkv, w_out, b_out, w_up, b_up, w_down, b_down, cotangent
):
    own_rows, width = inputs.shape
    units = w_up.shape[1]
    columns = w_qkv.shape[1]
    pairs = columns // TRIPLE
    piece_rows = w_up.shape[0]
    n_dp, n_tensor = lax.axis_size("dp"), lax.axis_size("tensor")
    by_hand = n_dp == 16 and n_tensor == 2
    block = min(UNIT_BLOCK, units)
    gains = jnp.stack([attn_gain, attn_bias, mlp_gain, mlp_bias])
    natural = jnp.arange(n_dp, dtype=jnp.int32)
    side = lax.axis_index("tensor").astype(jnp.int32)
    tables = rotary_tables(own_rows * n_tensor)

    def full_gather(piece):
        return lax.all_gather(piece, "dp", axis=0, tiled=True).reshape(n_dp, piece_rows, piece.shape[1])

    def full_scatter(parts):
        return lax.psum_scatter(parts.reshape(width, parts.shape[2]), "dp", scatter_dimension=0, tiled=True)

    biases = jnp.stack([b_out, b_down])
    if by_hand:
        sides = jnp.zeros((n_dp,), jnp.int32).at[0].set(side).at[1].set(1 - side)
        arrive, leave = relative_order((1, 2)), relative_order((2, 1))
        place = side[None]
        piece_a, piece_b, attn_piece = interleave(
            [(w_up, w_down.T, block, block), (w_qkv, w_out.T, pairs // 2 * TRIPLE, pairs // 2 * PAIR)], (2, 1)
        )
        first = pairs // 2
        later = (pairs - first) * PAIR
        x_other = swap_tensor(inputs)
        out_other = swap_tensor(w_out.T[:, first * PAIR :])
        lines_a = gather_lines(piece_a, x_other, out_other)
        held_dy, piece_b = hold([cotangent, piece_b], lines_a)
        dy_other = swap_tensor(held_dy)
        lines_b = gather_lines(piece_b)
        n1, n2, n1t, n2t, hat = two_sided(norm_kernel, place, inputs, x_other, [gains], (2, 1), 2)
        attn_piece = jnp.concatenate([attn_piece, out_other], axis=1)
        across_a, lines_b, attn_piece = hold([swap_dp(lines_a, 2), lines_b, attn_piece], n1, dy_other)
        attn_wide = full_gather(attn_piece)
        attn_parts = [attn_wide]
        parts_a = [lines_a, swap_dp(lines_a, 1), across_a, swap_dp(across_a, 1)]
        dy, dyt, dy_sum = two_sided(turn_kernel, place, cotangent, dy_other, [], (1, 0), 1, 1)

        order = jnp.stack([arrive, natural])
        buffer, gb_a, branch, dn2 = mlp_call(
            order, n2, n2t, dy, dyt, b_up[None, : units // 2], parts_a, chunk=(0, 2), after=[lines_b]
        )
        (across_b,) = hold([swap_dp(lines_b, 2)], gb_a)
        parts_b = [lines_b, swap_dp(lines_b, 1), across_b, swap_dp(across_b, 1)]
        wide, gb_b, branch, share, sums_two = mlp_call(
            order, n2, n2t, dy, dyt, b_up[None, units // 2 :], parts_b, chunk=(1, 2), buffer=buffer,
            init=(branch, dn2), final=(hat, mlp_gain),
        )
        mlp_sum = full_scatter(wide)
        attn_order = jnp.stack([natural, leave, sides])
        keep_c, send_c, gb_c, dn1, branch_home, branch_away = attention_call(
            attn_order, n1, n1t, dy, dyt, tables, b_qkv[None], attn_parts, 2, 0, first, (branch,), own_rows
        )
        branch_other = swap_tensor(branch_away)
        low_c, high_c = add_split([(keep_c, swap_dp(send_c, 1))], (4, 4))
        keep_d, send_d, gb_d, sums_one, branch_home, share_home, *share_away, ctx_away = attention_call(
            attn_order, n1, n1t, dy, dyt, tables, b_qkv[None], attn_parts, 2, 1, pairs - first,
            (branch_home, dn1), own_rows, final=(share, hat, attn_gain), after=[high_c],
        )
        across_c, branch_other, ctx_away, send_d, gb_d, *share_away = hold(
            [swap_dp(high_c, 2), branch_other, ctx_away, send_d, gb_d, *share_away]
        )
        small = flatten_rows([gb_c, gb_d, gb_a, gb_b, sums_one, sums_two, dy_sum])
        across_d, keep_d, small_other = hold([swap_dp(send_d, 1), keep_d, swap_dp(small, 1)])
        low_d, high_d = add_split([(keep_d, across_d)], (4, 4))
        small = small + small_other
        share_first, ctx_away = hold([share_away[0], ctx_away], high_d)
        across_d, share_first, ctx_other, *small_others = hold(
            [
                swap_dp(high_d, 2), swap_tensor(share_first), swap_tensor(ctx_away),
                swap_dp(small, 4), swap_dp(small, 8), swap_dp(small, 12),
            ]
        )
        small = sum(small_others, small)
        lines = add_split([(low_c, across_c), (low_d, across_d)], (1, 1, 1, 1))
        sent = send_lines(lines)
        share_second, small = hold([share_away[1], small], *lines)
        output = finish_output(
            inputs, [branch_home, branch_other], biases, ctx_other, attn_wide.reshape(width, -1), columns + pairs * PAIR
        )
        share_second, small_other, *sent = hold(
            [swap_tensor(share_second), swap_dp(small, 2), *sent], output
        )
        small = small + small_other
        small = small + swap_tensor(jnp.where(jnp.arange(small.shape[1]) < columns + units, 0.0, small))
        grad_inputs = finish_input(inputs, cotangent, share_home, [share_first, share_second])
        (mlp_sum,) = hold([mlp_sum], grad_inputs)
        grad_up, grad_down_t = finish_weights([[mlp_sum]], block, block)
        attn_sources = [sent]
        small = small[0]
        tail = small[columns + units :]
    else:
        mlp_piece, attn_piece = interleave(
            [(w_up, w_down.T, block, block), (w_qkv, w_out.T, columns, pairs * PAIR)], (1, 1)
        )
        order = jnp.stack([natural, natural, jnp.zeros_like(natural)])
        x = lax.all_gather(inputs, "tensor", axis=0, tiled=True)
        dy = lax.all_gather(cotangent, "tensor", axis=0, tiled=True)
        mlp_parts = [full_gather(mlp_piece)]
        attn_parts = [full_gather(attn_piece)]
        rows = x.shape[0]
        place = jnp.zeros((1,), jnp.int32)
        n1, n2, n1t, n2t, hat = two_sided(
            norm_kernel, place, x[: rows // 2], x[rows // 2 :], [gains], (2, 1), 2
        )
        dy, dyt, _ = two_sided(turn_kernel, place, dy[: rows // 2], dy[rows // 2 :], [], (1, 0), 1, 1)
        wide, gb_up, branch, share, sums_two = mlp_call(
            order[:2], n2, n2t, dy, dyt, b_up[None], mlp_parts, final=(hat, mlp_gain)
        )
        narrow, gb_qkv, sums_one, branch, share = attention_call(
            order, n1, n1t, dy, dyt, tables, b_qkv[None], attn_parts, 1, 0, pairs, (branch,), rows,
            final=(share, hat, attn_gain),
        )
        grad_up, grad_down_t = finish_weights([[full_scatter(wide)]], block, block)
        attn_sources = [[full_scatter(narrow)]]
        share = lax.psum_scatter(share.astype(BF16), "tensor", scatter_dimension=0, tiled=True)
        branch = lax.psum_scatter(branch.astype(BF16), "tensor", scatter_dimension=0, tiled=True)
        output = finish_output(inputs, [branch], biases)
        grad_inputs = finish_input(inputs, cotangent, share, [])
        small = lax.psum(jnp.concatenate([gb_qkv[0], gb_up[0]]), "dp")
        own_sum = jnp.sum(cotangent.astype(F32), axis=0)
        tail = lax.psum(jnp.concatenate([sums_one.reshape(-1), sums_two.reshape(-1), own_sum]), ("dp", "tensor"))

    sums = tail.reshape(5, width)
    calls = 2 if by_hand else 1
    grad_qkv, grad_out_t = finish_weights(attn_sources, columns // calls, pairs // calls * PAIR)
    return (
        output,
        grad_inputs,
        sums[0],
        sums[1],
        sums[2],
        sums[3],
        grad_qkv,
        small[:columns],
        grad_out_t.T,
        sums[4],
        grad_up,
        small[columns : columns + units],
        grad_down_t.T,
        sums[4],
    )


def solution(mesh):
    rows = P(("dp", "tensor"), None)
    return jax.shard_map(
        on_device,
        mesh=mesh,
        in_specs=(
            rows, P(), P(), P(), P(), P("dp", "tensor"), P("tensor"), P("tensor", "dp"), P(),
            P("dp", "tensor"), P("tensor"), P("tensor", "dp"), P(), rows,
        ),
        out_specs=(
            rows, rows, P(), P(), P(), P(), P("dp", "tensor"), P("tensor"), P("tensor", "dp"), P(),
            P("dp", "tensor"), P("tensor"), P("tensor", "dp"), P(),
        ),
        check_vma=False,
    )
```

```python
import jax
import jax.numpy as jnp
import numpy as np
from jax import lax
from jax.experimental import pallas as pl
from jax.experimental.pallas import tpu as pltpu
from jax.sharding import PartitionSpec as P

HD = 64
ROT = 16
SEQ = 1024
EPSILON = 1e-05
PAIR = 2 * HD
TRIPLE = 6 * HD
BOTH = TRIPLE + PAIR
Q_BLOCK = 256
ROW_BLOCK = 256
UNIT_BLOCK = 512
VMEM_BYTES = 60 * 1024 * 1024
F32 = jnp.float32
BF16 = jnp.bfloat16
ANY = pl.BlockSpec(memory_space=pl.ANY)


def normalize(rows):
    average = jnp.mean(rows, axis=-1, keepdims=True)
    centered = rows - average
    spread = jnp.mean(centered * centered, axis=-1, keepdims=True)
    rate = lax.rsqrt(spread + EPSILON)
    return centered * rate, rate


def rotary_tables(count):
    positions = (np.arange(count) % SEQ).astype(np.float32)
    inverse = (10000.0 ** (-(2.0 * np.arange(ROT // 2)) / ROT)).astype(np.float32)
    angles = (positions[:, None] * inverse[None, :]).astype(np.float64)
    cosine, sine = np.cos(angles), np.sin(angles)
    none = np.zeros_like(sine)
    rest = np.zeros((count, HD - ROT))
    keep = np.concatenate([cosine, cosine, rest + 1.0], axis=1)
    down = np.concatenate([none, sine, rest], axis=1)
    up = np.concatenate([-sine, none, rest], axis=1)
    return tuple(jnp.asarray(np.concatenate([t, t], axis=1), F32) for t in (keep, down, up))


def nn(left, right):
    return jnp.dot(left, right, preferred_element_type=F32)


def nt(left, right):
    return lax.dot_general(left, right, (((1,), (1,)), ((), ())), preferred_element_type=F32)


class Copies:
    def __init__(self, sem):
        self.sem = sem
        self.count = 0
        self.open = []

    def start(self, source, target):
        copy = pltpu.make_async_copy(source, target, self.sem.at[self.count])
        self.count += 1
        copy.start()
        self.open.append(copy)
        return copy

    def rows_in(self, order, parts, columns, target, into):
        copies, at = [], 0
        for part in parts:
            count, rows, _ = part.shape
            for slot in range(count):
                place = pl.ds(pl.multiple_of(order[0, at + slot] * rows, rows), rows)
                copies.append(self.start(part.at[slot, :, columns], target.at[place, into]))
            at += count
        return copies

    def rows_out(self, order, source, outof, parts, columns):
        at = 0
        for part in parts:
            count, rows, _ = part.shape
            for slot in range(count):
                place = pl.ds(pl.multiple_of(order[1, at + slot] * rows, rows), rows)
                self.start(source.at[place, outof], part.at[slot, :, columns])
            at += count

    def wait(self, *copies):
        for copy in copies:
            if copy in self.open:
                self.open.remove(copy)
                copy.wait()

    def wait_all(self):
        self.wait(*list(self.open))


def whole(shape):
    return pl.BlockSpec(shape, lambda i, *_: (0,) * len(shape))


def once(shape):
    return pl.BlockSpec(shape, lambda i, *_: (0,) * len(shape), pipeline_mode=pl.Buffered(1))


def shape_of(shape, dtype):
    return jax.ShapeDtypeStruct(shape, dtype)


def norm_kernel(place, own, other, gains, normed_one, normed_two, one_t, two_t, hat):
    mine = pl.program_id(0) // (pl.num_programs(0) // 2) == place[0]
    rows = jnp.where(mine, own[...], other[...]).astype(F32)
    xhat, _ = normalize(rows)
    one = (xhat * gains[0:1, :] + gains[1:2, :]).astype(BF16)
    two = (xhat * gains[2:3, :] + gains[3:4, :]).astype(BF16)
    normed_one[...] = one
    normed_two[...] = two
    one_t[...] = one.T
    two_t[...] = two.T
    hat[...] = xhat.astype(BF16)


def turn_kernel(place, own, other, rows_out, turned, total):
    mine = pl.program_id(0) // (pl.num_programs(0) // 2) == place[0]
    rows = jnp.where(mine, own[...], other[...])
    rows_out[...] = rows
    turned[...] = rows.T

    @pl.when(pl.program_id(0) == 0)
    def _():
        total[...] = jnp.zeros_like(total)

    @pl.when(mine)
    def _():
        total[...] += jnp.sum(own[...].astype(F32), axis=0, keepdims=True)


def two_sided(kernel, place, own, other, extra, straight, flipped, summed=0):
    rows, width = own.shape
    steps = 2 * rows // ROW_BLOCK
    half = pl.BlockSpec((ROW_BLOCK, width), lambda i, *_: (i % (steps // 2), 0))
    row_spec = pl.BlockSpec((ROW_BLOCK, width), lambda i, *_: (i, 0))
    col_spec = pl.BlockSpec((width, ROW_BLOCK), lambda i, *_: (0, i))
    before, after = straight
    return pl.pallas_call(
        kernel,
        grid_spec=pltpu.PrefetchScalarGridSpec(
            num_scalar_prefetch=1,
            grid=(steps,),
            in_specs=[half, half] + [whole(e.shape) for e in extra],
            out_specs=[row_spec] * before + [col_spec] * flipped + [row_spec] * after + [whole((1, width))] * summed,
        ),
        out_shape=[shape_of((2 * rows, width), BF16)] * before
        + [shape_of((width, 2 * rows), BF16)] * flipped
        + [shape_of((2 * rows, width), BF16)] * after
        + [shape_of((1, width), F32)] * summed,
        compiler_params=pltpu.CompilerParams(vmem_limit_bytes=VMEM_BYTES),
        name=kernel.__name__,
    )(place, own, other, *extra)


def mlp_call(order, n2, n2t, dy, dyt, bias, parts, chunk=(0, 1), buffer=None, init=None, final=None, after=()):
    tokens, width = n2.shape
    _, rows, both = parts[0].shape
    units = both // 2
    block = min(UNIT_BLOCK, units)
    steps = units // block
    n_parts = len(parts)
    slots = sum(part.shape[0] for part in parts)
    chunks = [slice(start, start + ROW_BLOCK) for start in range(0, tokens, ROW_BLOCK)]

    def kernel(order, *refs):
        refs = list(refs)
        take = lambda n: [refs.pop(0) for _ in range(n)]
        take(0 if buffer is None else 1)
        n2_hbm, dy_hbm, n2t_hbm, dyt_hbm, bias = take(5)
        weights = take(n_parts)
        starts = take(2 if init is not None else 0)
        hat_hbm, gain = take(2) if final is not None else (None, None)
        take(len(after))
        grads, gbias, branch_hbm, dnormed_hbm = take(4)
        sums = take(1)[0] if final is not None else None
        n2, dy, n2t, dyt, w, act, dhid, gwide, branch, dnormed, sem = take(11)
        hat = take(1)[0] if final is not None else None
        copies = Copies(sem)
        up = [slice(2 * i * block, (2 * i + 1) * block) for i in range(steps)]
        down = [slice((2 * i + 1) * block, (2 * i + 2) * block) for i in range(steps)]
        unit = [slice(i * block, (i + 1) * block) for i in range(steps)]
        need_up, need_down = [], []
        for i in range(steps):
            need_up.append(copies.rows_in(order, weights, up[i], w, up[i]))
            if i == 0:
                need_up[0].append(copies.start(n2_hbm, n2))
            need_down.append(copies.rows_in(order, weights, down[i], w, down[i]))
            if i == 0:
                need_down[0].append(copies.start(dy_hbm, dy))
        begun = []
        if init is not None:
            begun += [copies.start(starts[0], branch), copies.start(starts[1], dnormed)]
        if final is not None:
            begun += [copies.start(hat_hbm, hat)]
        need_n2t, need_dyt = copies.start(n2t_hbm, n2t), copies.start(dyt_hbm, dyt)
        for i in range(steps):
            total = jnp.zeros((1, block), F32)
            copies.wait(*need_up[i])
            for index, at in enumerate(chunks):
                hidden = nn(n2[at, :], w[:, up[i]]) + bias[:, unit[i]]
                if index == 0:
                    copies.wait(*need_down[i])
                dactive = nn(dy[at, :], w[:, down[i]])
                below = 0.5 + 0.5 * lax.erf(hidden * 0.7071067811865476)
                density = jnp.exp(hidden * hidden * -0.5) * 0.3989422804014327
                dhidden = (dactive * (below + hidden * density)).astype(BF16)
                act[at, unit[i]] = (hidden * below).astype(BF16)
                dhid[at, unit[i]] = dhidden
                total += jnp.sum(dhidden.astype(F32), axis=0, keepdims=True)
            gbias[:, unit[i]] = total
        copies.wait(*begun)
        hat_sum = direct_sum = jnp.zeros((1, width), F32)
        for at in chunks:
            direct = sum(nt(dhid[at, unit[i]], w[:, up[i]]) for i in range(steps))
            mixed = sum(nt(act[at, unit[i]], w[:, down[i]]) for i in range(steps))
            if init is not None:
                direct = direct + dnormed[at, :]
                mixed = mixed + branch[at, :]
            if final is not None:
                hat_sum += jnp.sum(direct * hat[at, :].astype(F32), axis=0, keepdims=True)
                direct_sum += jnp.sum(direct, axis=0, keepdims=True)
                direct = direct * gain[...]
            dnormed[at, :] = direct
            branch[at, :] = mixed
            copies.start(dnormed.at[at, :], dnormed_hbm.at[at, :])
            copies.start(branch.at[at, :], branch_hbm.at[at, :])
        if final is not None:
            sums[0:1, :] = hat_sum
            sums[1:2, :] = direct_sum
        copies.wait(need_n2t, need_dyt)
        for i in range(steps):
            both_at = slice(2 * i * block, (2 * i + 2) * block)
            shifted = slice(chunk[0] * both + 2 * i * block, chunk[0] * both + (2 * i + 2) * block)
            gwide[:, up[i]] = nn(n2t[...], dhid[:, unit[i]]).astype(BF16)
            gwide[:, down[i]] = nn(dyt[...], act[:, unit[i]]).astype(BF16)
            copies.rows_out(order, gwide, both_at, [grads], shifted)
        copies.wait_all()

    square = (tokens, width)
    in_specs = [ANY] * 4 + [whole((1, units))] + [ANY] * n_parts
    operands = [n2, dy, n2t, dyt, bias, *parts]
    out_specs = [ANY, whole((1, units)), ANY, ANY]
    out_shape = [
        shape_of((slots, rows, both * chunk[1]), BF16),
        shape_of((1, units), F32), shape_of(square, F32), shape_of(square, F32),
    ]
    if buffer is not None:
        in_specs = [ANY] + in_specs
        operands = [buffer] + operands
    scratch = [
        pltpu.VMEM(square, BF16), pltpu.VMEM(square, BF16),
        pltpu.VMEM((width, tokens), BF16), pltpu.VMEM((width, tokens), BF16),
        pltpu.VMEM((width, both), BF16), pltpu.VMEM((tokens, units), BF16), pltpu.VMEM((tokens, units), BF16),
        pltpu.VMEM((width, both), BF16), pltpu.VMEM(square, F32), pltpu.VMEM(square, F32),
        pltpu.SemaphoreType.DMA((3 * slots * steps + 2 * len(chunks) + 8,)),
    ]
    if init is not None:
        in_specs += [ANY, ANY]
        operands += list(init)
    if final is not None:
        hat, gain = final
        in_specs += [ANY, whole((1, width))]
        operands += [hat, gain[None]]
        out_specs += [whole((2, width))]
        out_shape += [shape_of((2, width), F32)]
        scratch += [pltpu.VMEM(square, BF16)]
    in_specs += [ANY] * len(after)
    operands += list(after)
    return pl.pallas_call(
        kernel,
        grid_spec=pltpu.PrefetchScalarGridSpec(
            num_scalar_prefetch=1, grid=(1,), in_specs=in_specs, out_specs=out_specs, scratch_shapes=scratch
        ),
        out_shape=out_shape,
        input_output_aliases={} if buffer is None else {1: 0},
        compiler_params=pltpu.CompilerParams(vmem_limit_bytes=VMEM_BYTES),
        cost_estimate=pl.CostEstimate(
            flops=12 * tokens * width * units, transcendentals=2 * tokens * units, bytes_accessed=32 * tokens * width
        ),
        name="mlp_both_ways",
    )(order, *operands)


def attention_call(order, n1, n1t, dy, dyt, tables, bias, parts, outs, call, pairs, init, home_rows, final=None, after=()):
    tokens, width = n1.shape
    rows = parts[0].shape[1]
    n_parts = len(parts)
    slots = sum(part.shape[0] for part in parts) // outs
    half = ROT // 2
    away_rows = tokens - home_rows
    last = final is not None
    shared = away_rows > 0
    share_cuts = [0, away_rows // 4, away_rows]
    wide, narrow = pairs * TRIPLE, pairs * PAIR
    size = wide + narrow
    chunks = [slice(start, start + ROW_BLOCK) for start in range(0, tokens, ROW_BLOCK)]

    def kernel(order, *refs):
        refs = list(refs)
        take = lambda n: [refs.pop(0) for _ in range(n)]
        n1_hbm, dy_hbm, n1t_hbm, dyt_hbm, keep, down, up, bias = take(8)
        weights = take(n_parts)
        starts = take(len(init))
        share_hbm, hat_hbm, gain = take(3) if last else (None, None, None)
        take(len(after))
        grads = take(outs)
        (gbias,) = take(1)
        if last:
            sums, branch_hbm, share_home = take(3)
            outs_away = take(3) if shared else []
        else:
            dnormed_hbm, branch_hbm, outs_away = take(2) + [take(1)]
        n1, dy, n1t, dyt, w, turned, dctx, ctx_t, dq_t, dkv, dmixed, context, gwide, dnormed, branch, sem = take(16)
        away_low = take(1)[0] if shared else None
        share, hat = take(2) if last else (None, None)
        home = pl.multiple_of(order[2, 0] * home_rows, home_rows)
        away = pl.multiple_of(order[2, 1] * away_rows, 16)
        copies = Copies(sem)
        everything = slice(0, size)
        need_w = copies.rows_in(order, weights, slice(call * size, (call + 1) * size), w, everything)
        need_n1 = copies.start(n1_hbm, n1)
        need_dy = copies.start(dy_hbm, dy)
        begun = [copies.start(start, total) for start, total in zip(starts, (branch, dnormed))]
        if last:
            begun += [copies.start(share_hbm, share), copies.start(hat_hbm, hat)]
        need_t = [copies.start(n1t_hbm, n1t), copies.start(dyt_hbm, dyt)]

        def rotate(rows, at, sign):
            lane = lax.broadcasted_iota(jnp.int32, rows[0].shape, 1)
            groups = []
            for index, r in enumerate(rows):
                shift = pltpu.roll(r, half, 1) * down[at, :] + pltpu.roll(r, PAIR - half, 1) * up[at, :]
                turn = r * keep[at, :] + sign * shift
                place = index % 3
                groups.append(turn if place == 0 else jnp.where((lane >= HD) == (place == 1), turn, r))
            return groups

        copies.wait(*need_w, need_n1)
        for at in chunks:
            mixed = nn(n1[at, :], w[:, :wide]) + bias[...]
            for index, group in enumerate(rotate([mixed[:, i * PAIR : (i + 1) * PAIR] for i in range(3 * pairs)], at, 1.0)):
                turned[at, index * PAIR : (index + 1) * PAIR] = group.astype(BF16)
        copies.wait(need_dy)
        dctx[...] = nn(dy[...], w[:, wide:]).astype(BF16)
        behind = lax.broadcasted_iota(jnp.int32, (Q_BLOCK, Q_BLOCK), 0) > lax.broadcasted_iota(
            jnp.int32, (Q_BLOCK, Q_BLOCK), 1
        )
        blank = jnp.zeros((tokens, HD), BF16)
        dkv[...] = jnp.zeros_like(dkv)
        for pair in range(pairs):
            heads = []
            for head in range(2):
                base = pair * TRIPLE + head * 3 * HD
                query = turned[:, base : base + HD] * jnp.asarray(0.125, BF16)
                key = turned[:, base + HD : base + 2 * HD]
                value = turned[:, base + 2 * HD : base + 3 * HD]
                grad = dctx[:, pair * PAIR + head * HD : pair * PAIR + (head + 1) * HD]
                left = jnp.concatenate([query, blank], axis=1)
                right = jnp.concatenate([blank, grad], axis=1)
                heads.append((query, key, value, grad, key.T, value.T, left, right))
            for start in range(0, tokens, Q_BLOCK):
                stop = start + Q_BLOCK
                products = [
                    (nt(key[:stop], query[start:stop]), nt(value[:stop], grad[start:stop]))
                    for query, key, value, grad, *_ in heads
                ]
                mixes = []
                for scores, dprobs in products:
                    edge = jnp.where(behind, -1e30, scores[start:])
                    scores = edge if start == 0 else jnp.concatenate([scores[:start], edge], axis=0)
                    expos = jnp.exp(scores - jnp.max(scores, axis=0, keepdims=True))
                    probs = expos * (1.0 / jnp.sum(expos, axis=0, keepdims=True))
                    inner = jnp.sum(probs * dprobs, axis=0, keepdims=True)
                    mixes.append((probs.astype(BF16), (probs * (dprobs - inner)).astype(BF16)))
                for head, (low, dscores) in enumerate(mixes):
                    _, _, _, _, key_t, value_t, left, right = heads[head]
                    lines = slice(pair * PAIR + head * HD, pair * PAIR + (head + 1) * HD)
                    ctx_t[lines, start:stop] = nn(value_t[:, :stop], low)
                    dq_t[lines, start:stop] = nn(key_t[:, :stop], dscores) * 0.125
                    dkv[2 * pair + head, :stop, :] += nn(dscores, left[start:stop]) + nn(low, right[start:stop])
        context[...] = ctx_t[...].T.astype(BF16)
        if shared and last:
            copies.start(context.at[pl.ds(away, away_rows), :], outs_away[2])
        copies.wait(*begun)
        total = jnp.zeros((1, wide), F32)
        hat_sum = direct_sum = jnp.zeros((1, width), F32)
        for at in chunks:
            rows_before = []
            lane = lax.broadcasted_iota(jnp.int32, (ROW_BLOCK, PAIR), 1)
            for pair in range(pairs):
                dq = dq_t[pair * PAIR : (pair + 1) * PAIR, at].T
                swapped = pltpu.roll(dkv[2 * pair, at, :], HD, 1)
                rows_before += [
                    jnp.where(lane < HD, dq, swapped), jnp.where(lane < HD, swapped, dq), dkv[2 * pair + 1, at, :]
                ]
            low = jnp.concatenate(rotate(rows_before, at, -1.0), axis=1).astype(BF16)
            dmixed[at, :] = low
            total += jnp.sum(low.astype(F32), axis=0, keepdims=True)
            direct = nt(low, w[:, :wide])
            if len(init) > 1:
                direct = direct + dnormed[at, :]
            if last:
                hat_sum += jnp.sum(direct * hat[at, :].astype(F32), axis=0, keepdims=True)
                direct_sum += jnp.sum(direct, axis=0, keepdims=True)
                direct = direct * gain[...] + share[at, :]
            dnormed[at, :] = direct
            if not last:
                copies.start(dnormed.at[at, :], dnormed_hbm.at[at, :])
        gbias[...] = total
        if last:
            sums[0:1, :] = hat_sum
            sums[1:2, :] = direct_sum
            copies.start(dnormed.at[pl.ds(home, home_rows), :], share_home)
            if shared:
                away_low[...] = dnormed[pl.ds(away, away_rows), :].astype(BF16)
                for index in range(2):
                    copies.start(away_low.at[share_cuts[index] : share_cuts[index + 1], :], outs_away[index])
            branch[...] += nt(context[pl.ds(home, home_rows), :], w[:, wide:])
            copies.start(branch, branch_hbm)
        else:
            branch[...] += nt(context[...], w[:, wide:])
            copies.start(branch.at[pl.ds(home, home_rows), :], branch_hbm)
            away_low[...] = branch[pl.ds(away, away_rows), :].astype(BF16)
            copies.start(away_low, outs_away[0])
        copies.wait(*need_t)
        gwide[:, wide:] = nn(dyt[...], context[...]).astype(BF16)
        gwide[:, :wide] = nn(n1t[...], dmixed[...]).astype(BF16)
        copies.rows_out(order, gwide, everything, grads, everything)
        copies.wait_all()

    square = (tokens, width)
    table = whole((tokens, PAIR))
    home, away = (home_rows, width), (away_rows, width)
    in_specs = [ANY] * 4 + [table] * 3 + [pl.BlockSpec((1, wide), lambda i, *_: (0, call))] + [ANY] * (n_parts + len(init))
    operands = [n1, dy, n1t, dyt, *tables, bias, *parts, *init]
    out_specs = [ANY] * outs + [whole((1, wide))]
    out_shape = [shape_of((slots, rows, size), BF16)] * outs + [shape_of((1, wide), F32)]
    scratch = [
        pltpu.VMEM(square, BF16), pltpu.VMEM(square, BF16),
        pltpu.VMEM((width, tokens), BF16), pltpu.VMEM((width, tokens), BF16),
        pltpu.VMEM((width, size), BF16), pltpu.VMEM((tokens, wide), BF16), pltpu.VMEM((tokens, narrow), BF16),
        pltpu.VMEM((narrow, tokens), F32), pltpu.VMEM((narrow, tokens), F32),
        pltpu.VMEM((2 * pairs, tokens, PAIR), F32), pltpu.VMEM((tokens, wide), BF16), pltpu.VMEM((tokens, narrow), BF16),
        pltpu.VMEM((width, size), BF16), pltpu.VMEM(square, F32), pltpu.VMEM(home if last else square, F32),
        pltpu.SemaphoreType.DMA((2 * slots * outs + len(chunks) + 16,)),
    ]
    if shared:
        scratch += [pltpu.VMEM(away, BF16)]
    if last:
        share, hat, gain = final
        in_specs += [ANY, ANY, whole((1, width))]
        operands += [share, hat, gain[None]]
        out_specs += [whole((2, width)), ANY, ANY]
        out_shape += [shape_of((2, width), F32), shape_of(home, F32), shape_of(home, F32)]
        if shared:
            out_specs += [ANY] * 3
            out_shape += [shape_of((share_cuts[i + 1] - share_cuts[i], width), BF16) for i in range(2)]
            out_shape += [shape_of((away_rows, narrow), BF16)]
        scratch += [pltpu.VMEM(square, F32), pltpu.VMEM(square, BF16)]
    else:
        out_specs += [ANY] * 3
        out_shape += [shape_of(square, F32), shape_of(home, F32), shape_of(away, BF16)]
    in_specs += [ANY] * len(after)
    operands += list(after)
    return pl.pallas_call(
        kernel,
        grid_spec=pltpu.PrefetchScalarGridSpec(
            num_scalar_prefetch=1, grid=(1,), in_specs=in_specs, out_specs=out_specs, scratch_shapes=scratch
        ),
        out_shape=out_shape,
        compiler_params=pltpu.CompilerParams(vmem_limit_bytes=VMEM_BYTES),
        cost_estimate=pl.CostEstimate(
            flops=pairs * 20 * tokens * width * BOTH, transcendentals=pairs * tokens * tokens,
            bytes_accessed=32 * tokens * width,
        ),
        name="attention_both_ways",
    )(order, *operands)


def swap_dp(array, bits):
    count = lax.axis_size("dp")
    return lax.ppermute(array, "dp", [(i, i ^ bits) for i in range(count)])


def swap_tensor(array):
    return lax.ppermute(array, "tensor", [(0, 1), (1, 0)])


def hold(arrays, *after):
    def kernel(*refs):
        del refs

    return pl.pallas_call(
        kernel,
        in_specs=[ANY] * (len(arrays) + len(after)),
        out_specs=[ANY] * len(arrays),
        out_shape=[shape_of(a.shape, a.dtype) for a in arrays],
        input_output_aliases={i: i for i in range(len(arrays))},
        name="hold",
    )(*arrays, *after)


def join(pieces, *after):
    rows, width = pieces[0].shape
    block = min(width, 1024)
    count = len(pieces)

    def kernel(*refs):
        out = refs[-1]
        for index in range(count):
            out[index] = refs[index][...]

    return pl.pallas_call(
        kernel,
        grid=(width // block,),
        in_specs=[pl.BlockSpec((rows, block), lambda i: (0, i))] * count + [ANY] * len(after),
        out_specs=pl.BlockSpec((count, rows, block), lambda i: (0, 0, i)),
        out_shape=shape_of((count, rows, width), BF16),
        name="join",
    )(*pieces, *after)


def interleave(pairs, chunks):
    rows = pairs[0][0].shape[0]
    layouts = []
    for (one, other, size_one, size_other), count in zip(pairs, chunks):
        steps = one.shape[1] // size_one // count
        layouts.append((size_one, size_other, steps, count))

    def kernel(*refs):
        ins, outs = refs[: 2 * len(pairs)], list(refs[2 * len(pairs) :])
        for index, (size_one, size_other, steps, count) in enumerate(layouts):
            one, other = ins[2 * index : 2 * index + 2]
            size = size_one + size_other
            for chunk in range(count):
                out = outs.pop(0)
                for step in range(steps):
                    at = chunk * steps + step
                    out[:, step * size : step * size + size_one] = one[:, at * size_one : (at + 1) * size_one]
                    out[:, step * size + size_one : (step + 1) * size] = other[:, at * size_other : (at + 1) * size_other]

    return pl.pallas_call(
        kernel,
        out_shape=[
            shape_of((rows, steps * (size_one + size_other)), BF16)
            for size_one, size_other, steps, count in layouts
            for _ in range(count)
        ],
        name="interleave",
    )(*[array for pair in pairs for array in pair[:2]])


def finish_weights(sources, size_one, size_other):
    size = size_one + size_other
    counts = [len(source) for source in sources]
    widths = [source[0].shape[-1] for source in sources]
    arrays = [array.reshape(array.shape[-2:]) for source in sources for array in source]
    rows = arrays[0].shape[0]
    steps = sum(widths) // size

    def kernel(*refs):
        ins, one, other = list(refs[:-2]), refs[-2], refs[-1]
        at = 0
        for count, width in zip(counts, widths):
            total = ins.pop(0)[...].astype(F32)
            for _ in range(count - 1):
                total = total + ins.pop(0)[...].astype(F32)
            for step in range(width // size):
                base = step * size
                one[:, at * size_one : (at + 1) * size_one] = total[:, base : base + size_one]
                other[:, at * size_other : (at + 1) * size_other] = total[:, base + size_one : base + size]
                at += 1

    return pl.pallas_call(
        kernel,
        out_shape=[shape_of((rows, steps * size_one), F32), shape_of((rows, steps * size_other), F32)],
        name="finish_weights",
    )(*arrays)


def finish_output(inputs, branches, biases, context=None, weights=None, column=0):
    rows, width = inputs.shape
    block = min(rows, 256)
    n_branches = len(branches)
    inner = 0 if context is None else context.shape[1]

    def kernel(x, bias, *refs):
        total = x[...].astype(F32) + bias[0:1, :] + bias[1:2, :]
        for ref in refs[:n_branches]:
            total = total + ref[...].astype(F32)
        if inner:
            total = total + nt(refs[n_branches][...], refs[n_branches + 1][...])
        refs[-1][...] = total.astype(BF16)

    spec = pl.BlockSpec((block, width), lambda i: (i, 0))
    in_specs = [spec, pl.BlockSpec((2, width), lambda i: (0, 0))] + [spec] * n_branches
    operands = [inputs, biases, *branches]
    if inner:
        in_specs += [
            pl.BlockSpec((block, inner), lambda i: (i, 0)), pl.BlockSpec((width, inner), lambda i: (0, column // inner))
        ]
        operands += [context, weights]
    return pl.pallas_call(
        kernel,
        grid=(rows // block,),
        in_specs=in_specs,
        out_specs=spec,
        out_shape=shape_of((rows, width), BF16),
        name="finish_output",
    )(*operands)


def finish_input(inputs, cotangent, home, others, *after):
    rows, width = inputs.shape
    block = min([rows, 128] + [other.shape[0] for other in others])
    starts = np.cumsum([0] + [other.shape[0] // block for other in others])
    count = len(others)

    def kernel(x, dy, home, *refs):
        step = pl.program_id(0)
        share = home[...].astype(F32)
        for index in range(count):
            mine = (step >= starts[index]) & (step < starts[index + 1])
            share = share + jnp.where(mine, refs[index][...].astype(F32), 0.0)
        xhat, rate = normalize(x[...].astype(F32))
        lead = jnp.mean(share, axis=-1, keepdims=True)
        along = jnp.mean(share * xhat, axis=-1, keepdims=True)
        refs[-1][...] = dy[...].astype(F32) + rate * (share - lead - xhat * along)

    def part(index):
        low, high = int(starts[index]), int(starts[index + 1])
        return pl.BlockSpec((block, width), lambda i: (jnp.clip(i - low, 0, high - low - 1), 0))

    spec = pl.BlockSpec((block, width), lambda i: (i, 0))
    return pl.pallas_call(
        kernel,
        grid=(rows // block,),
        in_specs=[spec] * 3 + [part(index) for index in range(count)] + [ANY] * len(after),
        out_specs=spec,
        out_shape=shape_of((rows, width), F32),
        name="finish_input",
    )(inputs, cotangent, home, *others, *after)


def flatten_rows(arrays):
    total = sum(a.shape[0] * a.shape[1] for a in arrays)

    def kernel(*refs):
        out, at = refs[-1], 0
        for ref in refs[:-1]:
            count, width = ref.shape
            for row in range(count):
                out[:, at : at + width] = ref[row : row + 1, :]
                at += width

    return pl.pallas_call(kernel, out_shape=shape_of((1, total), F32), name="flatten_rows")(*arrays)


def add_split(pairs, sizes):
    count, rows, width = pairs[0][0].shape
    block = min(width, 512)
    steps = width // block

    def kernel(*refs):
        ins, outs = refs[: 2 * len(pairs)], refs[2 * len(pairs) :]
        for index in range(len(pairs)):
            left, right = ins[2 * index : 2 * index + 2]

            @pl.when(pl.program_id(0) // steps == index)
            def _():
                at = 0
                for size, out in zip(sizes, outs):
                    total = left[at : at + size].astype(F32) + right[at : at + size].astype(F32)
                    out[...] = total.astype(BF16)
                    at += size

    def part(index):
        return pl.BlockSpec((count, rows, block), lambda i: (0, 0, jnp.clip(i - index * steps, 0, steps - 1)))

    return pl.pallas_call(
        kernel,
        grid=(len(pairs) * steps,),
        in_specs=[part(index) for index in range(len(pairs)) for _ in range(2)],
        out_specs=[pl.BlockSpec((size, rows, block), lambda i: (0, 0, i)) for size in sizes],
        out_shape=[shape_of((size, rows, len(pairs) * width), BF16) for size in sizes],
        name="add_split",
    )(*[array for pair in pairs for array in pair])


def relative_order(weights):
    slots = np.arange(16)
    bits = (slots % 4) * 4 + (slots // 4 % 2) * weights[0] + (slots // 8) * weights[1]
    return jnp.asarray(bits, jnp.int32) ^ lax.axis_index("dp").astype(jnp.int32)


def gather_lines(piece, *after):
    return join([piece] + [swap_dp(piece, 4 * s) for s in (1, 2, 3)], *after)


def send_lines(lines):
    return [lines[0]] + [swap_dp(lines[s], 4 * s) for s in (1, 2, 3)]


def on_device(
    inputs, attn_gain, attn_bias, mlp_gain, mlp_bias, w_qkv, b_qkv, w_out, b_out, w_up, b_up, w_down, b_down, cotangent
):
    own_rows, width = inputs.shape
    units = w_up.shape[1]
    columns = w_qkv.shape[1]
    pairs = columns // TRIPLE
    piece_rows = w_up.shape[0]
    n_dp, n_tensor = lax.axis_size("dp"), lax.axis_size("tensor")
    by_hand = n_dp == 16 and n_tensor == 2
    block = min(UNIT_BLOCK, units)
    gains = jnp.stack([attn_gain, attn_bias, mlp_gain, mlp_bias])
    natural = jnp.arange(n_dp, dtype=jnp.int32)
    side = lax.axis_index("tensor").astype(jnp.int32)
    tables = rotary_tables(own_rows * n_tensor)

    def full_gather(piece):
        return lax.all_gather(piece, "dp", axis=0, tiled=True).reshape(n_dp, piece_rows, piece.shape[1])

    def full_scatter(parts):
        return lax.psum_scatter(parts.reshape(width, parts.shape[2]), "dp", scatter_dimension=0, tiled=True)

    biases = jnp.stack([b_out, b_down])
    if by_hand:
        sides = jnp.zeros((n_dp,), jnp.int32).at[0].set(side).at[1].set(1 - side)
        arrive, leave = relative_order((1, 2)), relative_order((2, 1))
        place = side[None]
        piece_a, piece_b, attn_piece = interleave(
            [(w_up, w_down.T, block, block), (w_qkv, w_out.T, pairs // 2 * TRIPLE, pairs // 2 * PAIR)], (2, 1)
        )
        first = pairs // 2
        later = (pairs - first) * PAIR
        x_other = swap_tensor(inputs)
        out_other = swap_tensor(w_out.T[:, first * PAIR :])
        lines_a = gather_lines(piece_a, x_other, out_other)
        held_dy, piece_b = hold([cotangent, piece_b], lines_a)
        dy_other = swap_tensor(held_dy)
        lines_b = gather_lines(piece_b)
        n1, n2, n1t, n2t, hat = two_sided(norm_kernel, place, inputs, x_other, [gains], (2, 1), 2)
        attn_piece = jnp.concatenate([attn_piece, out_other], axis=1)
        across_a, lines_b, attn_piece = hold([swap_dp(lines_a, 2), lines_b, attn_piece], n1, dy_other)
        attn_wide = full_gather(attn_piece)
        attn_parts = [attn_wide]
        parts_a = [lines_a, swap_dp(lines_a, 1), across_a, swap_dp(across_a, 1)]
        dy, dyt, dy_sum = two_sided(turn_kernel, place, cotangent, dy_other, [], (1, 0), 1, 1)

        order = jnp.stack([arrive, natural])
        buffer, gb_a, branch, dn2 = mlp_call(
            order, n2, n2t, dy, dyt, b_up[None, : units // 2], parts_a, chunk=(0, 2), after=[lines_b]
        )
        (across_b,) = hold([swap_dp(lines_b, 2)], gb_a)
        parts_b = [lines_b, swap_dp(lines_b, 1), across_b, swap_dp(across_b, 1)]
        wide, gb_b, branch, share, sums_two = mlp_call(
            order, n2, n2t, dy, dyt, b_up[None, units // 2 :], parts_b, chunk=(1, 2), buffer=buffer,
            init=(branch, dn2), final=(hat, mlp_gain),
        )
        mlp_sum = full_scatter(wide)
        attn_order = jnp.stack([natural, leave, sides])
        keep_c, send_c, gb_c, dn1, branch_home, branch_away = attention_call(
            attn_order, n1, n1t, dy, dyt, tables, b_qkv[None], attn_parts, 2, 0, first, (branch,), own_rows
        )
        branch_other = swap_tensor(branch_away)
        low_c, high_c = add_split([(keep_c, swap_dp(send_c, 1))], (4, 4))
        keep_d, send_d, gb_d, sums_one, branch_home, share_home, *share_away, ctx_away = attention_call(
            attn_order, n1, n1t, dy, dyt, tables, b_qkv[None], attn_parts, 2, 1, pairs - first,
            (branch_home, dn1), own_rows, final=(share, hat, attn_gain), after=[high_c],
        )
        across_c, branch_other, ctx_away, send_d, gb_d, *share_away = hold(
            [swap_dp(high_c, 2), branch_other, ctx_away, send_d, gb_d, *share_away]
        )
        small = flatten_rows([gb_c, gb_d, gb_a, gb_b, sums_one, sums_two, dy_sum])
        across_d, keep_d, small_other = hold([swap_dp(send_d, 1), keep_d, swap_dp(small, 1)])
        low_d, high_d = add_split([(keep_d, across_d)], (4, 4))
        small = small + small_other
        share_first, ctx_away = hold([share_away[0], ctx_away], high_d)
        across_d, share_first, ctx_other, *small_others = hold(
            [
                swap_dp(high_d, 2), swap_tensor(share_first), swap_tensor(ctx_away),
                swap_dp(small, 4), swap_dp(small, 8), swap_dp(small, 12),
            ]
        )
        small = sum(small_others, small)
        lines = add_split([(low_c, across_c), (low_d, across_d)], (1, 1, 1, 1))
        sent = send_lines(lines)
        share_second, small = hold([share_away[1], small], *lines)
        output = finish_output(
            inputs, [branch_home, branch_other], biases, ctx_other, attn_wide.reshape(width, -1), columns + pairs * PAIR
        )
        grad_inputs = finish_input(inputs, cotangent, share_home, [share_first, swap_tensor(share_second)])
        small_other, *sent = hold([swap_dp(small, 2), *sent], output, grad_inputs)
        small = small + small_other
        small = small + swap_tensor(jnp.where(jnp.arange(small.shape[1]) < columns + units, 0.0, small))
        (mlp_sum,) = hold([mlp_sum], sent[0])
        grad_up, grad_down_t = finish_weights([[mlp_sum]], block, block)
        attn_sources = [sent]
        small = small[0]
        tail = small[columns + units :]
    else:
        mlp_piece, attn_piece = interleave(
            [(w_up, w_down.T, block, block), (w_qkv, w_out.T, columns, pairs * PAIR)], (1, 1)
        )
        order = jnp.stack([natural, natural, jnp.zeros_like(natural)])
        x = lax.all_gather(inputs, "tensor", axis=0, tiled=True)
        dy = lax.all_gather(cotangent, "tensor", axis=0, tiled=True)
        mlp_parts = [full_gather(mlp_piece)]
        attn_parts = [full_gather(attn_piece)]
        rows = x.shape[0]
        place = jnp.zeros((1,), jnp.int32)
        n1, n2, n1t, n2t, hat = two_sided(
            norm_kernel, place, x[: rows // 2], x[rows // 2 :], [gains], (2, 1), 2
        )
        dy, dyt, _ = two_sided(turn_kernel, place, dy[: rows // 2], dy[rows // 2 :], [], (1, 0), 1, 1)
        wide, gb_up, branch, share, sums_two = mlp_call(
            order[:2], n2, n2t, dy, dyt, b_up[None], mlp_parts, final=(hat, mlp_gain)
        )
        narrow, gb_qkv, sums_one, branch, share = attention_call(
            order, n1, n1t, dy, dyt, tables, b_qkv[None], attn_parts, 1, 0, pairs, (branch,), rows,
            final=(share, hat, attn_gain),
        )
        grad_up, grad_down_t = finish_weights([[full_scatter(wide)]], block, block)
        attn_sources = [[full_scatter(narrow)]]
        share = lax.psum_scatter(share.astype(BF16), "tensor", scatter_dimension=0, tiled=True)
        branch = lax.psum_scatter(branch.astype(BF16), "tensor", scatter_dimension=0, tiled=True)
        output = finish_output(inputs, [branch], biases)
        grad_inputs = finish_input(inputs, cotangent, share, [])
        small = lax.psum(jnp.concatenate([gb_qkv[0], gb_up[0]]), "dp")
        own_sum = jnp.sum(cotangent.astype(F32), axis=0)
        tail = lax.psum(jnp.concatenate([sums_one.reshape(-1), sums_two.reshape(-1), own_sum]), ("dp", "tensor"))

    sums = tail.reshape(5, width)
    calls = 2 if by_hand else 1
    grad_qkv, grad_out_t = finish_weights(attn_sources, columns // calls, pairs // calls * PAIR)
    return (
        output,
        grad_inputs,
        sums[0],
        sums[1],
        sums[2],
        sums[3],
        grad_qkv,
        small[:columns],
        grad_out_t.T,
        sums[4],
        grad_up,
        small[columns : columns + units],
        grad_down_t.T,
        sums[4],
    )


def solution(mesh):
    rows = P(("dp", "tensor"), None)
    return jax.shard_map(
        on_device,
        mesh=mesh,
        in_specs=(
            rows, P(), P(), P(), P(), P("dp", "tensor"), P("tensor"), P("tensor", "dp"), P(),
            P("dp", "tensor"), P("tensor"), P("tensor", "dp"), P(), rows,
        ),
        out_specs=(
            rows, rows, P(), P(), P(), P(), P("dp", "tensor"), P("tensor"), P("tensor", "dp"), P(),
            P("dp", "tensor"), P("tensor"), P("tensor", "dp"), P(),
        ),
        check_vma=False,
    )
```
